256 devices in a mesh: tm: 16 (over z, y_hi), gz: 16 (over y_lo, x, core).
Axes of the slice: x: 4, y: 4 (y_hi: 2, y_lo: 2; y = y_hi * 2 + y_lo), z: 8, core: 2. Of those that a mesh axis runs over, the one named last changes fastest.
Arguments:
- latent_start: float32 [8, 64, 8, 128], P(None, 'gz'), may hold values from -33 to 33
- noise_draws: bfloat16 [16, 8, 64, 8, 128], P('tm', None, 'gz'), may hold values from -4 to 4
- time_embed: float32 [16, 32], P('tm'), may hold values from -4 to 4
- step_scale: float32 [16], P('tm'), may hold values from 0.1 to 0.5
- noise_scale: float32 [16], P('tm'), may hold values from 0.05 to 0.3
- w_in: bfloat16 [32, 8, 3, 3, 3], replicated, may hold values from -0.4375 to 0.4375
- b_in: float32 [32], replicated, may hold values from -4 to 4
- gain_in: float32 [32], replicated, may hold values from 0.5 to 1.5
- shift_in: float32 [32], replicated, may hold values from -2 to 2
- w_mid: bfloat16 [32, 32, 3, 3, 3], replicated, may hold values from -0.21875 to 0.21875
- b_mid: float32 [32], replicated, may hold values from -4 to 4
- gain_mid: float32 [32], replicated, may hold values from 0.5 to 1.5
- shift_mid: float32 [32], replicated, may hold values from -2 to 2
- w_out: bfloat16 [8, 32, 3, 3, 3], replicated, may hold values from -0.21875 to 0.21875
- b_out: float32 [8], replicated, may hold values from -1.2 to 1.2
Outputs:
- trajectory: float32 [16, 8, 64, 8, 128], P('tm', None, 'gz')
The draws below stay inside these ranges and needn't reach their ends.
All inputs are finite; a program needn't handle non-finite values.
Results may differ from the reference program's by a relative error of at most 0.00073.
Values may be sent and summed in bfloat16 or wider, within the bound.
A program may use at most 64 MiB of HBM per device.

```python
import math
import jax
import jax.numpy as jnp
from jax import lax

CHANNELS = 8
FEATURES = 32
GROUPS = 8
EXTENT = 128
ROWS = 8
SWEEPS = 2
WINDOW = 16
Z_EXTENT = 64


def draw_latent_start(key, part):
    key = jax.random.fold_in(key, 17)
    key_base, key_offset = jax.random.split(key, 2)
    shape_full = (CHANNELS, Z_EXTENT, ROWS, EXTENT)
    planes_index = jnp.arange(Z_EXTENT, dtype=jnp.float32)
    plane_scale = 0.5 * jnp.exp(math.log(10.0) * planes_index / (Z_EXTENT - 1))
    rough_part = jnp.clip(jax.random.normal(key_base, shape_full, jnp.float32), -3.5, 3.5)
    offset = jnp.clip(0.8 * jax.random.normal(key_offset, (CHANNELS, 1, 1, 1), jnp.float32), -2.0, 2.0)
    return plane_scale[None, :, None, None] * (rough_part + offset)


def steps_of(rng, dims, cuts, low, high):
    def one(axis_at, shards_of):
        draws = jax.random.uniform(jax.random.fold_in(jax.random.fold_in(rng, 6), axis_at), (shards_of,), jnp.float32, low / len(cuts), high / len(cuts))
        return jnp.repeat(jnp.exp(draws), dims[axis_at] // shards_of).reshape((-1,) + (1,) * (len(dims) - axis_at - 1))

    gain = one(*cuts[0])
    for cut in cuts[1:]:
        gain = gain * one(*cut)
    return gain


def centred(own_key, shape, scale, bound, cuts=(), held_as=jnp.bfloat16):
    gain = steps_of(own_key, shape, cuts, -0.22, 0.18) if cuts else 1.0
    entries = jax.random.normal(own_key, shape, jnp.float32) * scale * gain
    return jnp.minimum(jnp.maximum(entries, -bound), bound).astype(held_as)


def setup_inputs(seed: int = 0) -> dict:
    streams_of = jax.random.split(jax.random.key(seed), 16)
    return {
        "latent_start": draw_latent_start(jax.random.fold_in(streams_of[15], 71), 0),
        "noise_draws": centred(streams_of[1], (WINDOW, CHANNELS, Z_EXTENT, ROWS, EXTENT), 1.0, 4.0, ((0, 16), (2, 16))),
        "time_embed": centred(streams_of[2], (WINDOW, FEATURES), 1.0, 4.0, ((0, 16),), jnp.float32),
        "step_scale": jnp.clip(jnp.exp(math.log(0.5) - 1.609438 * jax.random.uniform(streams_of[3], (WINDOW,), jnp.float32) ** steps_of(streams_of[3], (WINDOW,), ((0, 16),), -0.2, 0.2)), 0.1, 0.5),
        "noise_scale": jnp.clip(jnp.exp(math.log(0.3) - 1.7917595 * jax.random.uniform(streams_of[4], (WINDOW,), jnp.float32) ** steps_of(streams_of[4], (WINDOW,), ((0, 16),), -0.2, 0.2)), 0.05, 0.3),
        "w_in": centred(streams_of[5], (FEATURES, CHANNELS, 3, 3, 3), (27 * CHANNELS) ** -0.5, 0.4375),
        "b_in": centred(streams_of[6], (FEATURES,), 1.0, 4.0, (), jnp.float32),
        "gain_in": jnp.clip(jax.random.uniform(streams_of[7], (FEATURES,), jnp.float32, 0.5, 1.5), 0.5, 1.5),
        "shift_in": centred(streams_of[8], (FEATURES,), 0.5, 2.0, (), jnp.float32),
        "w_mid": centred(streams_of[9], (FEATURES, FEATURES, 3, 3, 3), (27 * FEATURES) ** -0.5, 0.21875),
        "b_mid": centred(streams_of[10], (FEATURES,), 1.0, 4.0, (), jnp.float32),
        "gain_mid": jnp.clip(jax.random.uniform(streams_of[11], (FEATURES,), jnp.float32, 0.5, 1.5), 0.5, 1.5),
        "shift_mid": centred(streams_of[12], (FEATURES,), 0.5, 2.0, (), jnp.float32),
        "w_out": centred(streams_of[13], (CHANNELS, FEATURES, 3, 3, 3), (27 * FEATURES) ** -0.5, 0.21875),
        "b_out": centred(streams_of[14], (CHANNELS,), 0.3, 1.2, (), jnp.float32),
    }


def periodic_conv(volume, weight):
    volume = lax.optimization_barrier(volume)
    padded = jnp.pad(volume.astype(jnp.float32), ((0, 0), (1, 1), (1, 1), (1, 1)), mode='wrap')
    result = lax.conv_general_dilated(padded[None], weight.astype(jnp.float32), (1, 1, 1), 'VALID', dimension_numbers=('NCDHW', 'OIDHW', 'NCDHW'), precision=lax.Precision.HIGHEST)
    return result[0]

def group_norm(features_map, gain_vec, shift_vec):
    grouped = features_map.reshape((GROUPS, FEATURES // GROUPS) + features_map.shape[1:])
    group_mean = lax.optimization_barrier(jnp.mean(grouped, axis=(1, 2, 3, 4), keepdims=True))
    group_var = lax.optimization_barrier(jnp.mean(jnp.square(grouped - group_mean), axis=(1, 2, 3, 4), keepdims=True))
    normed = ((grouped - group_mean) * lax.rsqrt(group_var + 1e-05)).reshape(features_map.shape)
    return normed * gain_vec[:, None, None, None] + shift_vec[:, None, None, None]

def column(vector):
    return vector[:, None, None, None]

def drift_of(current, embed_row, step_row, noise_row, draws_row, params):
    w_in, b_in, gain_in, shift_in, w_mid, b_mid, gain_mid, shift_mid, w_out, b_out = params
    lifted = periodic_conv(current.astype(jnp.bfloat16), w_in) + column(b_in) + column(embed_row)
    act_first = jax.nn.silu(group_norm(lifted, gain_in, shift_in)).astype(jnp.bfloat16)
    summed = periodic_conv(act_first, w_mid) + column(b_mid) + lifted
    act_second = jax.nn.silu(group_norm(summed, gain_mid, shift_mid)).astype(jnp.bfloat16)
    predicted = periodic_conv(act_second, w_out) + column(b_out)
    return step_row * predicted + noise_row * draws_row.astype(jnp.float32)

def reference(latent_start, noise_draws, time_embed, step_scale, noise_scale, w_in, b_in, gain_in, shift_in, w_mid, b_mid, gain_mid, shift_mid, w_out, b_out):
    params = (w_in, b_in, gain_in, shift_in, w_mid, b_mid, gain_mid, shift_mid, w_out, b_out)
    states = jnp.broadcast_to(latent_start, (WINDOW,) + latent_start.shape)
    for sweep_index in range(SWEEPS):
        increments = lax.map(lambda packed: drift_of(packed[0], packed[1], packed[2], packed[3], packed[4], params), (states, time_embed, step_scale, noise_scale, noise_draws))
        prefix = jnp.concatenate([jnp.zeros_like(increments[:1]), jnp.cumsum(increments[:-1], axis=0)], axis=0)
        if sweep_index + 1 < SWEEPS:
            states = latent_start[None] + prefix
    return latent_start[None] + prefix + increments
```

```python
import functools

import jax
import jax.numpy as jnp
from jax import lax
from jax.experimental import pallas as pl
from jax.experimental.pallas import tpu as pltpu
from jax.sharding import PartitionSpec as P

MESH = pl.DeviceIdType.MESH
F32, BF16 = jnp.float32, jnp.bfloat16
CH, FT, GR = 8, 32, 8
NY, NX, NZ = 8, 128, 4
SIDE = 16
HALO = 3
CELLS = (FT // GR) * NZ * NY * NX

GZ_ORDER = (12, 13, 4, 5, 8, 9, 14, 15, 10, 11, 2, 3, 6, 7, 1)
TM_ORDER = (
    (4, 1), (3, 1), (5, 1), (4, 0), (2, 1), (6, 1), (3, 0), (5, 0),
    (1, 1), (7, 1), (2, 0), (6, 0), (0, 1), (1, 0), (7, 0),
)


def flip(place, bits):
    for bit in (1, 2, 4, 8):
        if bits & bit:
            place = place + bit - 2 * bit * lax.rem(lax.div(place, bit), 2)
    return place


def shifted(place, steps, other):
    z, half = lax.div(place, 2), lax.rem(place, 2)
    if other:
        half = 1 - half
    return 2 * lax.rem(z + steps, SIDE // 2) + half


def unfold(count):
    row = lax.broadcasted_iota(jnp.int32, (count, 8 * count), 0)
    lane = lax.broadcasted_iota(jnp.int32, (count, 8 * count), 1)
    return (lax.div(lane, 8) == row).astype(F32).astype(BF16)


def tap_masks(lanes):
    y = lax.broadcasted_iota(jnp.int32, (8, lanes), 0)
    yin = lax.rem(lax.broadcasted_iota(jnp.int32, (8, lanes), 1), 8)
    return [yin == lax.rem(y + b + 7, 8) for b in range(3)]


def circulant(rows, masks):
    n, lanes = rows[0].shape
    out = jnp.zeros((n, 8, lanes), F32)
    for row, mask in zip(rows, masks):
        full = jnp.broadcast_to(row[:, None, :], (n, 8, lanes))
        out = jnp.where(jnp.broadcast_to(mask[None], (n, 8, lanes)), full, out)
    return out.reshape(8 * n, lanes)


def kernel(
    lat_ref, noise_ref, emb_ref, step_ref, nsc_ref, win_ref, bin_ref, gin_ref, sin_ref,
    wmid_ref, bmid_ref, gmid_ref, smid_ref, wout_ref, bout_ref,
    out_ref,
    vext, shift_in, lifted, act, summed, actb, a_in, a_mid, a_out, x_mid, splat, splat_out,
    stat, recv, send1, lat_chunk, chunk_a, chunk_b,
    halo_ss, halo_rs, stat_ss, stat_rs, p1_ss, p1_rs, p2_ss, p2_rs,
):
    k = lax.axis_index("tm")
    g = lax.axis_index("gz")
    up, down = lax.rem(g + 1, SIDE), lax.rem(g + SIDE - 1, SIDE)
    gz_peers = [flip(g, bits) for bits in GZ_ORDER]
    tm_peers = [shifted(k, steps, other) for steps, other in TM_ORDER]
    my_z, my_p = lax.div(k, 4), lax.rem(k, 4)
    pending = []

    barrier = pltpu.get_barrier_semaphore()
    for peer in tm_peers:
        pl.semaphore_signal(barrier, inc=1, device_id={"tm": peer}, device_id_type=MESH)
    for peer in gz_peers:
        pl.semaphore_signal(barrier, inc=1, device_id={"gz": peer}, device_id_type=MESH)

    for z in range(NZ):
        plane = lat_ref[:, z].reshape(CH * NY, NX)
        vext[0, HALO + z] = plane.reshape(4, 16, NX).astype(BF16)
        lat_chunk[4 * z : 4 * z + 4] = plane.reshape(4, 2, NY, NX)

    def mid_rows():
        x_mid[...] = jnp.dot(wmid_ref[...], unfold(FT), preferred_element_type=F32)
        masks = tap_masks(256)
        for a in range(3):
            for block in range(12):
                rows = [x_mid[(a * 3 + b) * 96 + 8 * block : (a * 3 + b) * 96 + 8 * block + 8, :] for b in range(3)]
                a_mid[64 * block : 64 * block + 64, 256 * a : 256 * a + 256] = circulant(rows, masks).astype(BF16)

    mid_rows()
    masks = tap_masks(256)
    x_out = jnp.dot(wout_ref[...], unfold(FT), preferred_element_type=F32)
    for a in range(3):
        rows = [x_out[(a * 3 + b) * 24 : (a * 3 + b) * 24 + 24] for b in range(3)]
        a_out[:, 256 * a : 256 * a + 256] = circulant(rows, masks).astype(BF16)
    masks = tap_masks(576)
    rows = []
    for b in range(3):
        w_b = jnp.concatenate([win_ref[(a * 3 + b) * 24 : (a * 3 + b) * 24 + 24, :].astype(F32) for a in range(3)], axis=0)
        rows.append(jnp.dot(w_b.T.astype(BF16), unfold(72), preferred_element_type=F32))
    for block in range(4):
        part = [row[8 * block : 8 * block + 8] for row in rows]
        a_in[64 * block : 64 * block + 64, :] = circulant(part, masks).astype(BF16)

    def spread(o, carry):
        at = pl.ds(o * 8 if isinstance(o, int) else pl.multiple_of(o * 8, 8), 8)
        for i, value in enumerate((
            bin_ref[o] + emb_ref[0, o], gin_ref[o], sin_ref[o], bmid_ref[o], gmid_ref[o], smid_ref[o],
        )):
            splat[i, at, :] = jnp.full((8, NX), value, F32)
        return carry

    lax.fori_loop(0, FT, spread, 0)
    for o in range(CH):
        splat_out[8 * o : 8 * o + 8, :] = jnp.full((8, NX), bout_ref[o], F32)

    pl.semaphore_wait(barrier, 2 * (SIDE - 1))

    def send(src, dst, ss, rs, device):
        copy = pltpu.make_async_remote_copy(
            src_ref=src, dst_ref=dst, send_sem=ss, recv_sem=rs, device_id=device, device_id_type=MESH
        )
        copy.start()
        pending.append(copy)
        return copy

    def halos(sweep):
        copies = [
            send(vext.at[sweep, pl.ds(NZ, HALO)], vext.at[sweep, pl.ds(0, HALO)],
                 halo_ss.at[sweep, 0], halo_rs.at[sweep, 0], {"gz": up}),
            send(vext.at[sweep, pl.ds(HALO, HALO)], vext.at[sweep, pl.ds(HALO + NZ, HALO)],
                 halo_ss.at[sweep, 1], halo_rs.at[sweep, 1], {"gz": down}),
        ]
        for copy in copies:
            copy.wait_recv()

    sub = lax.broadcasted_iota(jnp.int32, (8, NX), 0)
    low = lax.broadcasted_iota(jnp.int32, (8, NX), 1) < NX // 2

    def group_totals(ref, first, centre):
        totals = []
        for gr in range(GR):
            part = ref[32 * gr : 32 * gr + 32, first : first + NZ * NX]
            if centre is not None:
                part = part - centre[gr]
                part = part * part
            part = part.reshape(4, 8, NZ * NX)
            part = part[0] + part[1] + part[2] + part[3]
            part = part[:, :128] + part[:, 128:256] + part[:, 256:384] + part[:, 384:]
            part = jnp.sum(part, axis=0, keepdims=True)
            totals.append(jnp.sum(part, axis=1, keepdims=True))
        return totals

    def statistics(ref, first, turn):
        means = [t * (1.0 / CELLS) for t in group_totals(ref, first, None)]
        squares = group_totals(ref, first, means)
        tile = jnp.zeros((8, NX), F32)
        for gr in range(GR):
            both = jnp.where(low, jnp.broadcast_to(means[gr], (8, NX)), jnp.broadcast_to(squares[gr], (8, NX)))
            tile = jnp.where(sub == gr, both, tile)
        stat[turn] = tile
        recv[turn, g] = tile
        copies = []
        for i, peer in enumerate(gz_peers):
            copies.append(send(stat.at[turn], recv.at[turn, g], stat_ss.at[turn, i], stat_rs.at[turn, i], {"gz": peer}))
        for copy in copies:
            copy.wait_recv()
        every = recv[turn]
        total = jnp.sum(every, axis=0)
        mean = total * (1.0 / SIDE)
        off = every - mean[None]
        spread_of = jnp.sum(off * off, axis=0)
        var = (pltpu.roll(total, NX // 2, 1) + spread_of * CELLS) * (1.0 / (CELLS * SIDE))
        inv = lax.rsqrt(var + 1e-05)
        return jnp.where(low, mean, pltpu.roll(mean, NX // 2, 1)), jnp.where(low, inv, pltpu.roll(inv, NX // 2, 1))

    def normed(ref, gr, mean, inv, gain, shift):
        rows = ref[32 * gr : 32 * gr + 32, :]
        lanes = rows.shape[1]
        at = slice(32 * gr, 32 * gr + 32)
        m = jnp.broadcast_to(mean[gr : gr + 1], (32, NX))
        f = jnp.broadcast_to(inv[gr : gr + 1], (32, NX)) * splat[gain, at, :]
        s = splat[shift, at, :]
        tile = lambda t: jnp.concatenate([t] * (lanes // NX), axis=1)
        value = (rows - tile(m)) * tile(f) + tile(s)
        return value / (1.0 + jnp.exp(-value))

    step, noise_scale = step_ref[0], nsc_ref[0]

    for sweep in range(2):
        halos(sweep)
        for e in range(NZ + 2 * HALO):
            plane = vext[sweep, e].reshape(CH * NY, NX)
            wide = plane.astype(F32)
            at = slice(NX * e, NX * e + NX)
            shift_in[0:64, at] = pltpu.roll(wide, 1, 1).astype(BF16)
            shift_in[64:128, at] = plane
            shift_in[128:192, at] = pltpu.roll(wide, NX - 1, 1).astype(BF16)
        stacked = jnp.concatenate([shift_in[:, NX * a : NX * a + 1024] for a in range(3)], axis=0)
        lifted[...] = jnp.dot(a_in[...], stacked, preferred_element_type=F32) + jnp.concatenate([splat[0]] * 8, axis=1)

        mean, inv = statistics(lifted, 2 * NX, 2 * sweep)
        for gr in range(GR):
            act[32 * gr : 32 * gr + 32, :] = normed(lifted, gr, mean, inv, 1, 2).astype(BF16)
        stacked = jnp.concatenate([act[:, NX * a : NX * a + 768] for a in range(3)], axis=0)
        for part in range(4):
            at = slice(64 * part, 64 * part + 64)
            taps = [
                jnp.dot(a_mid[256 * c + 64 * part : 256 * c + 64 * part + 64, :], stacked, preferred_element_type=F32)
                for c in range(3)
            ]
            for z in range(NZ + 2):
                cut = slice(NX * z, NX * z + NX)
                summed[at, cut] = (
                    pltpu.roll(taps[0][:, cut], 1, 1) + taps[1][:, cut] + pltpu.roll(taps[2][:, cut], NX - 1, 1)
                    + splat[3, at, :] + lifted[at, NX * (z + 1) : NX * (z + 2)]
                )

        mean, inv = statistics(summed, NX, 2 * sweep + 1)
        for gr in range(GR):
            actb[32 * gr : 32 * gr + 32, :] = normed(summed, gr, mean, inv, 4, 5).astype(BF16)
        stacked = jnp.concatenate([actb[:, NX * a : NX * a + 512] for a in range(3)], axis=0)
        taps = jnp.dot(a_out[...], stacked, preferred_element_type=F32)
        for z in range(NZ):
            cut = slice(NX * z, NX * z + NX)
            predicted = (
                pltpu.roll(taps[0:64, cut], 1, 1) + taps[64:128, cut] + pltpu.roll(taps[128:192, cut], NX - 1, 1)
                + splat_out[...]
            )
            draws = noise_ref[:, z].astype(F32).reshape(CH * NY, NX)
            send1[sweep, 4 * z : 4 * z + 4] = (step * predicted + noise_scale * draws).reshape(4, 2, NY, NX)

        chunk_a[sweep, k] = send1[sweep, k]
        copies = []
        for i, peer in enumerate(tm_peers):
            copies.append(send(send1.at[sweep, peer], chunk_a.at[sweep, k], p1_ss.at[sweep, i], p1_rs.at[sweep, i], {"tm": peer}))
        for copy in copies:
            copy.wait_recv()
        state = lat_chunk[k]
        for s in range(SIDE):
            if sweep == 0:
                chunk_b[s] = state.reshape(16, NX).astype(BF16)
                state = state + chunk_a[sweep, s]
            else:
                state = state + chunk_a[sweep, s]
                recv_out = state
                send1[2, s] = recv_out
        copies = []
        for i, peer in enumerate(tm_peers):
            if sweep == 0:
                src, dst = chunk_b.at[peer], vext.at[1, HALO + my_z, my_p]
            else:
                src, dst = send1.at[2, peer], out_ref.at[pl.ds(2 * my_p, 2), my_z]
            copies.append(send(src, dst, p2_ss.at[sweep, i], p2_rs.at[sweep, i], {"tm": peer}))
        if sweep == 0:
            vext[1, HALO + my_z, my_p] = chunk_b[k]
        else:
            out_ref[pl.ds(2 * my_p, 2), my_z] = send1[2, k]
        for copy in copies:
            copy.wait_recv()

    for copy in pending:
        copy.wait_send()


def shards(
    latent_start, noise_draws, time_embed, step_scale, noise_scale, w_in, b_in, gain_in, shift_in,
    w_mid, b_mid, gain_mid, shift_mid, w_out, b_out,
):
    vmem, smem = pl.BlockSpec(memory_space=pltpu.VMEM), pl.BlockSpec(memory_space=pltpu.SMEM)
    dma = pltpu.SemaphoreType.DMA
    out = pl.pallas_call(
        kernel,
        out_shape=jax.ShapeDtypeStruct((CH, NZ, NY, NX), F32),
        in_specs=[vmem, vmem, smem, smem, smem, vmem, smem, smem, smem, vmem, smem, smem, smem, vmem, smem],
        out_specs=vmem,
        scratch_shapes=[
            pltpu.VMEM((2, NZ + 2 * HALO, 4, 16, NX), BF16),
            pltpu.VMEM((192, (NZ + 2 * HALO) * NX), BF16),
            pltpu.VMEM((256, 8 * NX), F32),
            pltpu.VMEM((256, 8 * NX), BF16),
            pltpu.VMEM((256, 6 * NX), F32),
            pltpu.VMEM((256, 6 * NX), BF16),
            pltpu.VMEM((256, 576), BF16),
            pltpu.VMEM((768, 768), BF16),
            pltpu.VMEM((192, 768), BF16),
            pltpu.VMEM((864, 256), F32),
            pltpu.VMEM((6, 256, NX), F32),
            pltpu.VMEM((64, NX), F32),
            pltpu.VMEM((4, 8, NX), F32),
            pltpu.VMEM((4, SIDE, 8, NX), F32),
            pltpu.VMEM((3, SIDE, 2, NY, NX), F32),
            pltpu.VMEM((SIDE, 2, NY, NX), F32),
            pltpu.VMEM((2, SIDE, 2, NY, NX), F32),
            pltpu.VMEM((SIDE, 16, NX), BF16),
            dma((2, 2)), dma((2, 2)), dma((4, SIDE)), dma((4, SIDE)),
            dma((2, SIDE)), dma((2, SIDE)), dma((2, SIDE)), dma((2, SIDE)),
        ],
        compiler_params=pltpu.CompilerParams(
            collective_id=0, has_side_effects=True, vmem_limit_bytes=40 * 2**20
        ),
    )(
        latent_start, noise_draws[0], time_embed, step_scale, noise_scale,
        w_in.transpose(2, 3, 4, 1, 0).reshape(27 * CH, FT), b_in, gain_in, shift_in,
        w_mid.transpose(2, 3, 4, 0, 1).reshape(27 * FT, FT), b_mid, gain_mid, shift_mid,
        w_out.transpose(2, 3, 4, 0, 1).reshape(27 * CH, FT), b_out,
    )
    return out[None]


def solution(mesh):
    in_specs = (
        P(None, "gz", None, None), P("tm", None, "gz", None, None), P("tm", None), P("tm"), P("tm"),
        P(), P(), P(), P(), P(), P(), P(), P(), P(), P(),
    )
    out_specs = P("tm", None, "gz", None, None)
    return jax.shard_map(shards, mesh=mesh, in_specs=in_specs, out_specs=out_specs, check_vma=False)
```

```python
import functools

import jax
import jax.numpy as jnp
from jax import lax
from jax.experimental import pallas as pl
from jax.experimental.pallas import tpu as pltpu
from jax.sharding import PartitionSpec as P

MESH = pl.DeviceIdType.MESH
F32, BF16 = jnp.float32, jnp.bfloat16
CH, FT, GR = 8, 32, 8
NY, NX, NZ = 8, 128, 4
SIDE = 16
HALO = 3
CELLS = (FT // GR) * NZ * NY * NX

GZ_ORDER = (12, 13, 4, 5, 8, 9, 14, 15, 10, 11, 2, 3, 6, 7, 1)
TM_ORDER = (
    (4, 1), (3, 1), (5, 1), (4, 0), (2, 1), (6, 1), (3, 0), (5, 0),
    (1, 1), (7, 1), (2, 0), (6, 0), (0, 1), (1, 0), (7, 0),
)


def flip(place, bits):
    for bit in (1, 2, 4, 8):
        if bits & bit:
            place = place + bit - 2 * bit * lax.rem(lax.div(place, bit), 2)
    return place


def shifted(place, steps, other):
    z, half = lax.div(place, 2), lax.rem(place, 2)
    if other:
        half = 1 - half
    return 2 * lax.rem(z + steps, SIDE // 2) + half


def unfold(count):
    row = lax.broadcasted_iota(jnp.int32, (count, 8 * count), 0)
    lane = lax.broadcasted_iota(jnp.int32, (count, 8 * count), 1)
    return (lax.div(lane, 8) == row).astype(F32).astype(BF16)


def tap_masks(lanes):
    y = lax.broadcasted_iota(jnp.int32, (8, lanes), 0)
    yin = lax.rem(lax.broadcasted_iota(jnp.int32, (8, lanes), 1), 8)
    return [yin == lax.rem(y + b + 7, 8) for b in range(3)]


def circulant(rows, masks):
    n, lanes = rows[0].shape
    out = jnp.zeros((n, 8, lanes), F32)
    for row, mask in zip(rows, masks):
        full = jnp.broadcast_to(row[:, None, :], (n, 8, lanes))
        out = jnp.where(jnp.broadcast_to(mask[None], (n, 8, lanes)), full, out)
    return out.reshape(8 * n, lanes)


def kernel(
    lat_hbm, noise_hbm, emb_hbm, step_hbm, nsc_hbm, win_hbm, bin_hbm, gin_hbm, sin_hbm,
    wmid_hbm, bmid_hbm, gmid_hbm, smid_hbm, wout_hbm, bout_hbm,
    out_ref,
    lat_ref, noise_ref, win_ref, wmid_ref, wout_ref, emb_ref, step_ref, nsc_ref,
    bin_ref, gin_ref, sin_ref, bmid_ref, gmid_ref, smid_ref, bout_ref,
    vext, shift_in, lifted, act, summed, actb, a_in, a_mid, a_out, x_mid, splat, splat_out,
    stat, recv, send1, lat_chunk, chunk_a, chunk_b,
    load_sem, halo_ss, halo_rs, stat_ss, stat_rs, p1_ss, p1_rs, p2_ss, p2_rs,
):
    k = lax.axis_index("tm")
    g = lax.axis_index("gz")
    up, down = lax.rem(g + 1, SIDE), lax.rem(g + SIDE - 1, SIDE)
    gz_peers = [flip(g, bits) for bits in GZ_ORDER]
    tm_peers = [shifted(k, steps, other) for steps, other in TM_ORDER]
    my_z, my_p = lax.div(k, 4), lax.rem(k, 4)
    pending = []

    barrier = pltpu.get_barrier_semaphore()
    for peer in tm_peers:
        pl.semaphore_signal(barrier, inc=1, device_id={"tm": peer}, device_id_type=MESH)
    for peer in gz_peers:
        pl.semaphore_signal(barrier, inc=1, device_id={"gz": peer}, device_id_type=MESH)

    loads = []
    for src, dst in (
        (lat_hbm, lat_ref), (wmid_hbm, wmid_ref), (wout_hbm, wout_ref), (win_hbm, win_ref), (emb_hbm, emb_ref),
        (bin_hbm, bin_ref), (gin_hbm, gin_ref), (sin_hbm, sin_ref), (bmid_hbm, bmid_ref), (gmid_hbm, gmid_ref),
        (smid_hbm, smid_ref), (bout_hbm, bout_ref), (step_hbm, step_ref), (nsc_hbm, nsc_ref), (noise_hbm, noise_ref),
    ):
        copy = pltpu.make_async_copy(src, dst, load_sem.at[len(loads)])
        copy.start()
        loads.append(copy)

    loads[0].wait()
    for z in range(NZ):
        plane = lat_ref[:, z].reshape(CH * NY, NX)
        vext[0, HALO + z] = plane.reshape(4, 16, NX).astype(BF16)
        lat_chunk[4 * z : 4 * z + 4] = plane.reshape(4, 2, NY, NX)

    loads[1].wait()
    x_mid[...] = jnp.dot(wmid_ref[...], unfold(FT), preferred_element_type=F32)
    masks = tap_masks(256)
    for a in range(3):
        for block in range(12):
            rows = [x_mid[(a * 3 + b) * 96 + 8 * block : (a * 3 + b) * 96 + 8 * block + 8, :] for b in range(3)]
            a_mid[64 * block : 64 * block + 64, 256 * a : 256 * a + 256] = circulant(rows, masks).astype(BF16)
    loads[2].wait()
    x_out = jnp.dot(wout_ref[...], unfold(FT), preferred_element_type=F32)
    for a in range(3):
        rows = [x_out[(a * 3 + b) * 24 : (a * 3 + b) * 24 + 24] for b in range(3)]
        a_out[:, 256 * a : 256 * a + 256] = circulant(rows, masks).astype(BF16)
    loads[3].wait()
    masks = tap_masks(576)
    rows = []
    for b in range(3):
        w_b = jnp.concatenate([win_ref[(a * 3 + b) * 24 : (a * 3 + b) * 24 + 24, :].astype(F32) for a in range(3)], axis=0)
        rows.append(jnp.dot(w_b.T.astype(BF16), unfold(72), preferred_element_type=F32))
    for block in range(4):
        part = [row[8 * block : 8 * block + 8] for row in rows]
        a_in[64 * block : 64 * block + 64, :] = circulant(part, masks).astype(BF16)

    for copy in loads[4:]:
        copy.wait()

    def spread(o, carry):
        at = pl.ds(pl.multiple_of(o * 8, 8), 8)
        for i, value in enumerate((
            bin_ref[o] + emb_ref[0, o], gin_ref[o], sin_ref[o], bmid_ref[o], gmid_ref[o], smid_ref[o],
        )):
            splat[i, at, :] = jnp.full((8, NX), value, F32)
        return carry

    lax.fori_loop(0, FT, spread, 0)
    for o in range(CH):
        splat_out[8 * o : 8 * o + 8, :] = jnp.full((8, NX), bout_ref[o], F32)
    step, noise_scale = step_ref[0], nsc_ref[0]

    pl.semaphore_wait(barrier, 2 * (SIDE - 1))

    def send(src, dst, ss, rs, device):
        copy = pltpu.make_async_remote_copy(
            src_ref=src, dst_ref=dst, send_sem=ss, recv_sem=rs, device_id=device, device_id_type=MESH
        )
        copy.start()
        pending.append(copy)
        return copy

    def lanes(first, count=1):
        return slice(NX * first, NX * (first + count))

    sub = lax.broadcasted_iota(jnp.int32, (8, NX), 0)
    low = lax.broadcasted_iota(jnp.int32, (8, NX), 1) < NX // 2

    def lane_sums(groups):
        rows = jnp.concatenate([jnp.sum(t, axis=0, keepdims=True) for t in groups], axis=0)
        return jnp.broadcast_to(jnp.sum(rows, axis=1, keepdims=True), (8, NX))

    def fold(ref, planes, centre=None):
        plain, squares = [], []
        for gr in range(GR):
            tiles = []
            for q in planes:
                for c in range(4):
                    tile = ref[32 * gr + 8 * c : 32 * gr + 8 * c + 8, lanes(q)]
                    tiles.append(tile if centre is None else tile - jnp.broadcast_to(centre[gr : gr + 1], (8, NX)))
            plain.append(functools.reduce(lambda x, y: x + y, tiles))
            if centre is not None:
                squares.append(functools.reduce(lambda x, y: x + y, [t * t for t in tiles]))
        return plain, squares

    def centre_of(ref, planes):
        return lane_sums(fold(ref, planes)[0]) * (1.0 / (len(planes) * 4 * NY * NX))

    def announce(ref, inner, outer, centre, turn):
        plain, squares = fold(ref, inner, centre)
        plain2, squares2 = fold(ref, outer, centre)
        first = lane_sums([x + y for x, y in zip(plain, plain2)])
        second = lane_sums([x + y for x, y in zip(squares, squares2)])
        off = first * (1.0 / CELLS)
        tile = jnp.where(low, centre + off, second - first * off)
        stat[turn] = tile
        recv[turn, g] = tile
        return [
            send(stat.at[turn], recv.at[turn, g], stat_ss.at[turn, i], stat_rs.at[turn, i], {"gz": peer})
            for i, peer in enumerate(gz_peers)
        ]

    def gathered(copies, turn):
        for copy in copies:
            copy.wait_recv()
        every = recv[turn]
        total = jnp.sum(every, axis=0)
        mean = total * (1.0 / SIDE)
        off = every - mean[None]
        spread_of = jnp.sum(off * off, axis=0)
        var = (pltpu.roll(total, NX // 2, 1) + spread_of * CELLS) * (1.0 / (CELLS * SIDE))
        inv = lax.rsqrt(var + 1e-05)
        return jnp.where(low, mean, pltpu.roll(mean, NX // 2, 1)), jnp.where(low, inv, pltpu.roll(inv, NX // 2, 1))

    def activate(src, dst, planes, mean, inv, gain, shift):
        for gr in range(GR):
            at = slice(32 * gr, 32 * gr + 32)
            m = jnp.broadcast_to(mean[gr : gr + 1], (32, NX))
            f = jnp.broadcast_to(inv[gr : gr + 1], (32, NX)) * splat[gain, at, :]
            s = splat[shift, at, :]
            for q in planes:
                value = (src[at, lanes(q)] - m) * f + s
                dst[at, lanes(q)] = (value / (1.0 + jnp.exp(-value))).astype(BF16)

    def stack(src, planes):
        return jnp.concatenate([jnp.concatenate([src[:, lanes(q + a)] for q in planes], axis=1) for a in range(3)], axis=0)

    def turned(sweep, planes):
        for e in planes:
            plane = vext[sweep, e].reshape(CH * NY, NX)
            wide = plane.astype(F32)
            shift_in[0:64, lanes(e)] = pltpu.roll(wide, 1, 1).astype(BF16)
            shift_in[64:128, lanes(e)] = plane
            shift_in[128:192, lanes(e)] = pltpu.roll(wide, NX - 1, 1).astype(BF16)

    def lift(planes):
        out = jnp.dot(a_in[...], stack(shift_in, planes), preferred_element_type=F32)
        for i, q in enumerate(planes):
            lifted[:, lanes(q)] = out[:, lanes(i)] + splat[0]

    def middle(planes):
        rhs = stack(act, planes)
        taps = jnp.dot(a_mid[...], rhs, preferred_element_type=F32)
        for i, r in enumerate(planes):
            summed[:, lanes(r)] = (
                pltpu.roll(taps[0:256, lanes(i)], 1, 1) + taps[256:512, lanes(i)]
                + pltpu.roll(taps[512:768, lanes(i)], NX - 1, 1) + splat[3] + lifted[:, lanes(r + 1)]
            )

    for sweep in range(2):
        halo = [
            send(vext.at[sweep, pl.ds(NZ, HALO)], vext.at[sweep, pl.ds(0, HALO)],
                 halo_ss.at[sweep, 0], halo_rs.at[sweep, 0], {"gz": up}),
            send(vext.at[sweep, pl.ds(HALO, HALO)], vext.at[sweep, pl.ds(HALO + NZ, HALO)],
                 halo_ss.at[sweep, 1], halo_rs.at[sweep, 1], {"gz": down}),
        ]
        turned(sweep, (3, 4, 5, 6))
        lift((3, 4))
        centre = centre_of(lifted, (3, 4))
        for copy in halo:
            copy.wait_recv()
        turned(sweep, (2, 7))
        lift((2, 5))
        copies = announce(lifted, (3, 4), (2, 5), centre, 2 * sweep)
        turned(sweep, (0, 1, 8, 9))
        lift((0, 1, 6, 7))
        mean, inv = gathered(copies, 2 * sweep)

        activate(lifted, act, (1, 2, 3, 4, 5, 6), mean, inv, 1, 2)
        middle((2, 3))
        centre = centre_of(summed, (2, 3))
        middle((1, 4))
        copies = announce(summed, (2, 3), (1, 4), centre, 2 * sweep + 1)
        activate(lifted, act, (0, 7), mean, inv, 1, 2)
        middle((0, 5))
        mean, inv = gathered(copies, 2 * sweep + 1)

        activate(summed, actb, range(6), mean, inv, 4, 5)
        taps = jnp.dot(a_out[...], stack(actb, range(NZ)), preferred_element_type=F32)
        for z in range(NZ):
            predicted = (
                pltpu.roll(taps[0:64, lanes(z)], 1, 1) + taps[64:128, lanes(z)]
                + pltpu.roll(taps[128:192, lanes(z)], NX - 1, 1) + splat_out[...]
            )
            draws = noise_ref[:, z].astype(F32).reshape(CH * NY, NX)
            send1[sweep, 4 * z : 4 * z + 4] = (step * predicted + noise_scale * draws).reshape(4, 2, NY, NX)

        chunk_a[sweep, k] = send1[sweep, k]
        copies = [
            send(send1.at[sweep, peer], chunk_a.at[sweep, k], p1_ss.at[sweep, i], p1_rs.at[sweep, i], {"tm": peer})
            for i, peer in enumerate(tm_peers)
        ]
        for copy in copies:
            copy.wait_recv()
        state = lat_chunk[k]
        for s in range(SIDE):
            if sweep == 0:
                chunk_b[s] = state.reshape(16, NX).astype(BF16)
            state = state + chunk_a[sweep, s]
            if sweep == 1:
                send1[2, s] = state
        copies = []
        for i, peer in enumerate(tm_peers):
            if sweep == 0:
                src, dst = chunk_b.at[peer], vext.at[1, HALO + my_z, my_p]
            else:
                src, dst = send1.at[2, peer], out_ref.at[pl.ds(2 * my_p, 2), my_z]
            copies.append(send(src, dst, p2_ss.at[sweep, i], p2_rs.at[sweep, i], {"tm": peer}))
        if sweep == 0:
            vext[1, HALO + my_z, my_p] = chunk_b[k]
        else:
            out_ref[pl.ds(2 * my_p, 2), my_z] = send1[2, k]
        for copy in copies:
            copy.wait_recv()

    for copy in pending:
        copy.wait_send()


def shards(
    latent_start, noise_draws, time_embed, step_scale, noise_scale, w_in, b_in, gain_in, shift_in,
    w_mid, b_mid, gain_mid, shift_mid, w_out, b_out,
):
    vmem = pl.BlockSpec(memory_space=pltpu.VMEM)
    params = [pltpu.SMEM((FT,), F32)] * 6
    dma = pltpu.SemaphoreType.DMA
    out = pl.pallas_call(
        kernel,
        out_shape=pltpu.VMEM((CH, NZ, NY, NX), F32),
        in_specs=[pl.BlockSpec(memory_space=pltpu.HBM)] * 15,
        out_specs=vmem,
        scratch_shapes=[
            pltpu.VMEM((CH, NZ, NY, NX), F32), pltpu.VMEM((CH, NZ, NY, NX), BF16),
            pltpu.VMEM((27 * CH, FT), BF16), pltpu.VMEM((27 * FT, FT), BF16), pltpu.VMEM((27 * CH, FT), BF16),
            pltpu.SMEM((1, FT), F32), pltpu.SMEM((1,), F32), pltpu.SMEM((1,), F32), *params, pltpu.SMEM((CH,), F32),
            pltpu.VMEM((2, NZ + 2 * HALO, 4, 16, NX), BF16),
            pltpu.VMEM((192, (NZ + 2 * HALO) * NX), BF16),
            pltpu.VMEM((256, 8 * NX), F32),
            pltpu.VMEM((256, 8 * NX), BF16),
            pltpu.VMEM((256, 6 * NX), F32),
            pltpu.VMEM((256, 6 * NX), BF16),
            pltpu.VMEM((256, 576), BF16),
            pltpu.VMEM((768, 768), BF16),
            pltpu.VMEM((192, 768), BF16),
            pltpu.VMEM((864, 256), F32),
            pltpu.VMEM((6, 256, NX), F32),
            pltpu.VMEM((64, NX), F32),
            pltpu.VMEM((4, 8, NX), F32),
            pltpu.VMEM((4, SIDE, 8, NX), F32),
            pltpu.VMEM((3, SIDE, 2, NY, NX), F32),
            pltpu.VMEM((SIDE, 2, NY, NX), F32),
            pltpu.VMEM((2, SIDE, 2, NY, NX), F32),
            pltpu.VMEM((SIDE, 16, NX), BF16),
            dma((15,)), dma((2, 2)), dma((2, 2)), dma((4, SIDE)), dma((4, SIDE)),
            dma((2, SIDE)), dma((2, SIDE)), dma((2, SIDE)), dma((2, SIDE)),
        ],
        compiler_params=pltpu.CompilerParams(
            collective_id=0, has_side_effects=True, vmem_limit_bytes=60 * 2**20
        ),
    )(
        latent_start, noise_draws[0], time_embed, step_scale, noise_scale,
        w_in.transpose(2, 3, 4, 1, 0).reshape(27 * CH, FT), b_in, gain_in, shift_in,
        w_mid.transpose(2, 3, 4, 0, 1).reshape(27 * FT, FT), b_mid, gain_mid, shift_mid,
        w_out.transpose(2, 3, 4, 0, 1).reshape(27 * CH, FT), b_out,
    )
    return out[None]


def solution(mesh):
    in_specs = (
        P(None, "gz", None, None), P("tm", None, "gz", None, None), P("tm", None), P("tm"), P("tm"),
        P(), P(), P(), P(), P(), P(), P(), P(), P(), P(),
    )
    out_specs = P("tm", None, "gz", None, None)
    return jax.shard_map(shards, mesh=mesh, in_specs=in_specs, out_specs=out_specs, check_vma=False)
```

```python
import functools

import jax
import jax.numpy as jnp
from jax import lax
from jax.experimental import pallas as pl
from jax.experimental.pallas import tpu as pltpu
from jax.sharding import PartitionSpec as P

MESH = pl.DeviceIdType.MESH
F32, BF16 = jnp.float32, jnp.bfloat16
CH, FT, GR = 8, 32, 8
NY, NX, NZ = 8, 128, 4
SIDE = 16
HALO = 3
CELLS = (FT // GR) * NZ * NY * NX

GZ_ORDER = (12, 13, 4, 5, 8, 9, 14, 15, 10, 11, 2, 3, 6, 7, 1)
TM_ORDER = (
    (4, 1), (3, 1), (5, 1), (4, 0), (2, 1), (6, 1), (3, 0), (5, 0),
    (1, 1), (7, 1), (2, 0), (6, 0), (0, 1), (1, 0), (7, 0),
)


def flip(place, bits):
    for bit in (1, 2, 4, 8):
        if bits & bit:
            place = place + bit - 2 * bit * lax.rem(lax.div(place, bit), 2)
    return place


def shifted(place, steps, other):
    z, half = lax.div(place, 2), lax.rem(place, 2)
    if other:
        half = 1 - half
    return 2 * lax.rem(z + steps, SIDE // 2) + half


def unfold(count):
    row = lax.broadcasted_iota(jnp.int32, (count, 8 * count), 0)
    lane = lax.broadcasted_iota(jnp.int32, (count, 8 * count), 1)
    return (lax.div(lane, 8) == row).astype(F32).astype(BF16)


def tap_masks(lanes):
    y = lax.broadcasted_iota(jnp.int32, (8, lanes), 0)
    yin = lax.rem(lax.broadcasted_iota(jnp.int32, (8, lanes), 1), 8)
    return [yin == lax.rem(y + b + 7, 8) for b in range(3)]


def circulant(rows, masks):
    n, lanes = rows[0].shape
    out = jnp.zeros((n, 8, lanes), F32)
    for row, mask in zip(rows, masks):
        full = jnp.broadcast_to(row[:, None, :], (n, 8, lanes))
        out = jnp.where(jnp.broadcast_to(mask[None], (n, 8, lanes)), full, out)
    return out.reshape(8 * n, lanes)


def kernel(
    lat_hbm, noise_hbm, emb_hbm, step_hbm, nsc_hbm, win_hbm, bin_hbm, gin_hbm, sin_hbm,
    wmid_hbm, bmid_hbm, gmid_hbm, smid_hbm, wout_hbm, bout_hbm,
    out_ref,
    lat_ref, noise_ref, win_ref, wmid_ref, wout_ref, emb_ref, step_ref, nsc_ref,
    bin_ref, gin_ref, sin_ref, bmid_ref, gmid_ref, smid_ref, bout_ref,
    vext, shift_in, lifted, act, summed, actb, a_in, a_mid, a_out, x_mid, splat, splat_out, drift,
    stat, recv, send1, lat_chunk, chunk_a, chunk_b,
    relay_sem, load_sem, halo_ss, halo_rs, edge_ss, edge_rs, stat_ss, stat_rs, p1_ss, p1_rs, p2_ss, p2_rs,
):
    k = lax.axis_index("tm")
    g = lax.axis_index("gz")
    up, down = lax.rem(g + 1, SIDE), lax.rem(g + SIDE - 1, SIDE)
    gz_peers = [flip(g, bits) for bits in GZ_ORDER]
    tm_peers = [shifted(k, steps, other) for steps, other in TM_ORDER]
    my_z, my_p = lax.div(k, 4), lax.rem(k, 4)
    pending = []

    barrier = pltpu.get_barrier_semaphore()
    beside = [shifted(k, 1, 0), shifted(k, SIDE // 2 - 1, 0)]
    beyond = [shifted(k, 2, 0), shifted(k, SIDE // 2 - 2, 0)]
    across = [shifted(k, 0, 1)]
    for peer in beside + across:
        pl.semaphore_signal(barrier, inc=1, device_id={"tm": peer}, device_id_type=MESH)
    for peer in gz_peers:
        pl.semaphore_signal(barrier, inc=1, device_id={"gz": peer}, device_id_type=MESH)

    loads = []
    for src, dst in (
        (lat_hbm, lat_ref), (wmid_hbm, wmid_ref), (wout_hbm, wout_ref), (win_hbm, win_ref), (emb_hbm, emb_ref),
        (bin_hbm, bin_ref), (gin_hbm, gin_ref), (sin_hbm, sin_ref), (bmid_hbm, bmid_ref), (gmid_hbm, gmid_ref),
        (smid_hbm, smid_ref), (bout_hbm, bout_ref), (step_hbm, step_ref), (nsc_hbm, nsc_ref), (noise_hbm, noise_ref),
    ):
        copy = pltpu.make_async_copy(src, dst, load_sem.at[len(loads)])
        copy.start()
        loads.append(copy)

    loads[0].wait()
    for z in range(NZ):
        plane = lat_ref[:, z].reshape(CH * NY, NX)
        vext[0, HALO + z] = plane.reshape(4, 16, NX).astype(BF16)
        lat_chunk[4 * z : 4 * z + 4] = plane.reshape(4, 2, NY, NX)

    def load_mid():
        loads[1].wait()
        x_mid[...] = jnp.dot(wmid_ref[...], unfold(FT), preferred_element_type=F32)
        masks = tap_masks(256)
        for a in range(3):
            for block in range(12):
                first = a * 288 + 8 * block
                rows = [x_mid[first + 96 * b : first + 96 * b + 8, :] for b in range(3)]
                a_mid[64 * block : 64 * block + 64, 256 * a : 256 * a + 256] = circulant(rows, masks).astype(BF16)

    def load_out():
        loads[2].wait()
        masks = tap_masks(256)
        x_out = jnp.dot(wout_ref[...], unfold(FT), preferred_element_type=F32)
        for a in range(3):
            rows = [x_out[(a * 3 + b) * 24 : (a * 3 + b) * 24 + 24] for b in range(3)]
            a_out[:, 256 * a : 256 * a + 256] = circulant(rows, masks).astype(BF16)

    loads[3].wait()
    masks = tap_masks(576)
    rows = []
    for b in range(3):
        w_b = jnp.concatenate([win_ref[(a * 3 + b) * 24 : (a * 3 + b) * 24 + 24, :].astype(F32) for a in range(3)], axis=0)
        rows.append(jnp.dot(w_b.T.astype(BF16), unfold(72), preferred_element_type=F32))
    for block in range(4):
        part = [row[8 * block : 8 * block + 8] for row in rows]
        a_in[64 * block : 64 * block + 64, :] = circulant(part, masks).astype(BF16)

    for copy in loads[4:]:
        copy.wait()

    def spread(o, carry):
        at = pl.ds(pl.multiple_of(o * 8, 8), 8)
        for i, value in enumerate((
            bin_ref[o] + emb_ref[0, o], 0.5 * gin_ref[o], 0.5 * sin_ref[o],
            bmid_ref[o], 0.5 * gmid_ref[o], 0.5 * smid_ref[o],
        )):
            splat[i, at, :] = jnp.full((8, NX), value, F32)
        return carry

    lax.fori_loop(0, FT, spread, 0)
    for o in range(CH):
        splat_out[8 * o : 8 * o + 8, :] = jnp.full((8, NX), bout_ref[o], F32)
    step, noise_scale = step_ref[0], nsc_ref[0]

    pl.semaphore_wait(barrier, len(GZ_ORDER) + len(beside + across))

    def relay(turn, peers):
        for peer in peers:
            pl.semaphore_signal(relay_sem.at[turn], inc=1, device_id={"tm": peer}, device_id_type=MESH)

    relay(0, beside)

    def send(src, dst, ss, rs, device):
        copy = pltpu.make_async_remote_copy(
            src_ref=src, dst_ref=dst, send_sem=ss, recv_sem=rs, device_id=device, device_id_type=MESH
        )
        copy.start()
        pending.append(copy)
        return copy

    def settle(copies):
        fresh = {id(copy) for copy in copies}
        for copy in pending:
            if id(copy) not in fresh:
                copy.wait_send()
        pending[:] = copies
        for copy in copies:
            copy.wait_recv()

    def lanes(first, count=1):
        return slice(NX * first, NX * (first + count))

    sub = lax.broadcasted_iota(jnp.int32, (8, NX), 0)
    low = lax.broadcasted_iota(jnp.int32, (8, NX), 1) < NX // 2

    def lane_sums(groups):
        rows = jnp.concatenate([jnp.sum(t, axis=0, keepdims=True) for t in groups], axis=0)
        return jnp.broadcast_to(jnp.sum(rows, axis=1, keepdims=True), (8, NX))

    def fold(ref, planes, centre=None):
        plain, squares = [], []
        for gr in range(GR):
            tiles = []
            for q in planes:
                for c in range(4):
                    tile = ref[32 * gr + 8 * c : 32 * gr + 8 * c + 8, lanes(q)]
                    tiles.append(tile if centre is None else tile - jnp.broadcast_to(centre[gr : gr + 1], (8, NX)))
            plain.append(functools.reduce(lambda x, y: x + y, tiles))
            if centre is not None:
                squares.append(functools.reduce(lambda x, y: x + y, [t * t for t in tiles]))
        return plain, squares

    def centre_of(ref, planes):
        return lane_sums(fold(ref, planes)[0]) * (1.0 / (len(planes) * 4 * NY * NX))

    def announce(ref, inner, outer, centre, turn):
        plain, squares = fold(ref, inner, centre)
        plain2, squares2 = fold(ref, outer, centre)
        first = lane_sums([x + y for x, y in zip(plain, plain2)])
        second = lane_sums([x + y for x, y in zip(squares, squares2)])
        off = first * (1.0 / CELLS)
        tile = jnp.where(low, centre + off, second - first * off)
        stat[turn] = tile
        recv[turn, g] = tile
        return [
            send(stat.at[turn], recv.at[turn, g], stat_ss.at[turn, i], stat_rs.at[turn, i], {"gz": peer})
            for i, peer in enumerate(gz_peers)
        ]

    def gathered(copies, turn):
        settle(copies)
        every = recv[turn]
        total = jnp.sum(every, axis=0)
        mean = total * (1.0 / SIDE)
        off = every - mean[None]
        spread_of = jnp.sum(off * off, axis=0)
        var = (pltpu.roll(total, NX // 2, 1) + spread_of * CELLS) * (1.0 / (CELLS * SIDE))
        inv = lax.rsqrt(var + 1e-05)
        return jnp.where(low, mean, pltpu.roll(mean, NX // 2, 1)), jnp.where(low, inv, pltpu.roll(inv, NX // 2, 1))

    def activate(src, dst, planes, mean, inv, gain, shift):
        for gr in range(GR):
            at = slice(32 * gr, 32 * gr + 32)
            m = jnp.broadcast_to(mean[gr : gr + 1], (32, NX))
            f = jnp.broadcast_to(inv[gr : gr + 1], (32, NX)) * splat[gain, at, :]
            s = splat[shift, at, :]
            for q in planes:
                half = (src[at, lanes(q)] - m) * f + s
                dst[at, lanes(q)] = (half + half * jnp.tanh(half)).astype(BF16)

    def stack(src, planes):
        return jnp.concatenate([jnp.concatenate([src[:, lanes(q + a)] for q in planes], axis=1) for a in range(3)], axis=0)

    def turned(sweep, planes):
        for e in planes:
            plane = vext[sweep, e].reshape(CH * NY, NX)
            wide = plane.astype(F32)
            shift_in[0:64, lanes(e)] = pltpu.roll(wide, 1, 1).astype(BF16)
            shift_in[64:128, lanes(e)] = plane
            shift_in[128:192, lanes(e)] = pltpu.roll(wide, NX - 1, 1).astype(BF16)

    def lift(planes):
        out = jnp.dot(a_in[...], stack(shift_in, planes), preferred_element_type=F32)
        for i, q in enumerate(planes):
            lifted[:, lanes(q)] = out[:, lanes(i)] + splat[0]

    def middle(planes):
        rhs = stack(act, planes)
        taps = jnp.dot(a_mid[...], rhs, preferred_element_type=F32)
        for i, r in enumerate(planes):
            summed[:, lanes(r)] = (
                pltpu.roll(taps[0:256, lanes(i)], 1, 1) + taps[256:512, lanes(i)]
                + pltpu.roll(taps[512:768, lanes(i)], NX - 1, 1) + splat[3] + lifted[:, lanes(r + 1)]
            )

    for sweep in range(2):
        if sweep == 0:
            halo = [
                send(vext.at[0, pl.ds(NZ, HALO)], vext.at[0, pl.ds(0, HALO)],
                     halo_ss.at[0, 0], halo_rs.at[0, 0], {"gz": up}),
                send(vext.at[0, pl.ds(HALO, HALO)], vext.at[0, pl.ds(HALO + NZ, HALO)],
                     halo_ss.at[0, 1], halo_rs.at[0, 1], {"gz": down}),
            ]
            for z in range(NZ):
                draws = noise_ref[:, z].astype(F32).reshape(CH * NY, NX)
                drift[z] = step * splat_out[...] + noise_scale * draws
            turned(sweep, (3, 4, 5, 6))
            lift((3, 4))
            centre = centre_of(lifted, (3, 4))
            settle(halo)
            turned(sweep, (2, 7))
            lift((2, 5))
            copies = announce(lifted, (3, 4), (2, 5), centre, 0)
            pl.semaphore_wait(relay_sem.at[0], 2)
            relay(1, beyond)
            turned(sweep, (0, 1, 8, 9))
            lift((0, 1, 6, 7))
            load_mid()
        else:
            halo = [
                send(vext.at[1, pl.ds(NZ, 2)], vext.at[1, pl.ds(0, 2)],
                     halo_ss.at[1, 0], halo_rs.at[1, 0], {"gz": up}),
                send(vext.at[1, pl.ds(NZ, 2)], vext.at[1, pl.ds(HALO + NZ + 1, 2)],
                     halo_ss.at[1, 1], halo_rs.at[1, 1], {"gz": down}),
            ]
            turned(sweep, (2, 3, 4, 5, 6, 7))
            lift((2, 3, 4, 5))
            centre = centre_of(lifted, (3, 4))
            copies = announce(lifted, (3, 4), (2, 5), centre, 2)
            for copy in halo:
                copy.wait_recv()
            turned(sweep, (0, 1, 8, 9))
            lift((0, 1, 6, 7))
        mean, inv = gathered(copies, 2 * sweep)
        if sweep == 0:
            pl.semaphore_wait(relay_sem.at[1], 2)
            relay(2, across)

        activate(lifted, act, (1, 2, 3, 4, 5, 6), mean, inv, 1, 2)
        middle((2, 3))
        centre = centre_of(summed, (2, 3))
        middle((1, 4))
        copies = announce(summed, (2, 3), (1, 4), centre, 2 * sweep + 1)
        activate(lifted, act, (0, 7), mean, inv, 1, 2)
        middle((0, 5))
        if sweep == 0:
            load_out()
            pl.semaphore_wait(relay_sem.at[2], 1)
        mean, inv = gathered(copies, 2 * sweep + 1)

        activate(summed, actb, range(6), mean, inv, 4, 5)
        taps = jnp.dot(a_out[...], stack(actb, range(NZ)), preferred_element_type=F32)
        for z in range(NZ):
            predicted = (
                pltpu.roll(taps[0:64, lanes(z)], 1, 1) + taps[64:128, lanes(z)]
                + pltpu.roll(taps[128:192, lanes(z)], NX - 1, 1)
            )
            send1[sweep, 4 * z : 4 * z + 4] = (step * predicted + drift[z]).reshape(4, 2, NY, NX)

        chunk_a[sweep, k] = send1[sweep, k]
        copies = [
            send(send1.at[sweep, peer], chunk_a.at[sweep, k], p1_ss.at[sweep, i], p1_rs.at[sweep, i], {"tm": peer})
            for i, peer in enumerate(tm_peers)
        ]
        settle(copies)
        state = lat_chunk[k]
        for s in range(SIDE):
            if sweep == 0:
                chunk_b[s] = state.reshape(16, NX).astype(BF16)
            state = state + chunk_a[sweep, s]
            if sweep == 1:
                send1[2, s] = state
        copies = []
        if sweep == 0:
            face = (my_z == 0) | (my_z == NZ - 1)
            first = my_z == 0
            other, plane = jnp.where(first, down, up), jnp.where(first, HALO + NZ, HALO - 1)
            edge = jnp.where(first, 4, 0) + my_p

            def edge_copy(i, peer):
                return pltpu.make_async_remote_copy(
                    src_ref=chunk_b.at[peer], dst_ref=vext.at[1, plane, my_p], send_sem=edge_ss.at[i],
                    recv_sem=edge_rs.at[edge], device_id={"tm": peer, "gz": other}, device_id_type=MESH,
                )

            @pl.when(face)
            def _():
                for i, peer in enumerate(tm_peers + [k]):
                    edge_copy(i, peer).start()

        for i, peer in enumerate(tm_peers):
            if sweep == 0:
                src, dst = chunk_b.at[peer], vext.at[1, HALO + my_z, my_p]
            else:
                src, dst = send1.at[2, peer], out_ref.at[pl.ds(2 * my_p, 2), my_z]
            copies.append(send(src, dst, p2_ss.at[sweep, i], p2_rs.at[sweep, i], {"tm": peer}))
        if sweep == 0:
            vext[1, HALO + my_z, my_p] = chunk_b[k]
        else:
            out_ref[pl.ds(2 * my_p, 2), my_z] = send1[2, k]
        settle(copies)
        if sweep == 0:
            for i in range(8):
                pltpu.make_async_remote_copy(
                    src_ref=chunk_b.at[0], dst_ref=vext.at[1, HALO + NZ if i >= 4 else HALO - 1, i % 4],
                    send_sem=edge_ss.at[0], recv_sem=edge_rs.at[i], device_id={"gz": up}, device_id_type=MESH,
                ).wait_recv()

            @pl.when(face)
            def _():
                for i, peer in enumerate(tm_peers + [k]):
                    edge_copy(i, peer).wait_send()

    for copy in pending:
        copy.wait_send()


def shards(
    latent_start, noise_draws, time_embed, step_scale, noise_scale, w_in, b_in, gain_in, shift_in,
    w_mid, b_mid, gain_mid, shift_mid, w_out, b_out,
):
    vmem = pl.BlockSpec(memory_space=pltpu.VMEM)
    params = [pltpu.SMEM((FT,), F32)] * 6
    dma = pltpu.SemaphoreType.DMA
    out = pl.pallas_call(
        kernel,
        out_shape=pltpu.VMEM((CH, NZ, NY, NX), F32),
        in_specs=[pl.BlockSpec(memory_space=pltpu.HBM)] * 15,
        out_specs=vmem,
        scratch_shapes=[
            pltpu.VMEM((CH, NZ, NY, NX), F32), pltpu.VMEM((CH, NZ, NY, NX), BF16),
            pltpu.VMEM((27 * CH, FT), BF16), pltpu.VMEM((27 * FT, FT), BF16), pltpu.VMEM((27 * CH, FT), BF16),
            pltpu.SMEM((1, FT), F32), pltpu.SMEM((1,), F32), pltpu.SMEM((1,), F32), *params, pltpu.SMEM((CH,), F32),
            pltpu.VMEM((2, NZ + 2 * HALO, 4, 16, NX), BF16),
            pltpu.VMEM((192, (NZ + 2 * HALO) * NX), BF16),
            pltpu.VMEM((256, 8 * NX), F32),
            pltpu.VMEM((256, 8 * NX), BF16),
            pltpu.VMEM((256, 6 * NX), F32),
            pltpu.VMEM((256, 6 * NX), BF16),
            pltpu.VMEM((256, 576), BF16),
            pltpu.VMEM((768, 768), BF16),
            pltpu.VMEM((192, 768), BF16),
            pltpu.VMEM((864, 256), F32),
            pltpu.VMEM((6, 256, NX), F32),
            pltpu.VMEM((64, NX), F32),
            pltpu.VMEM((NZ, 64, NX), F32),
            pltpu.VMEM((4, 8, NX), F32),
            pltpu.VMEM((4, SIDE, 8, NX), F32),
            pltpu.VMEM((3, SIDE, 2, NY, NX), F32),
            pltpu.VMEM((SIDE, 2, NY, NX), F32),
            pltpu.VMEM((2, SIDE, 2, NY, NX), F32),
            pltpu.VMEM((SIDE, 16, NX), BF16),
            pltpu.SemaphoreType.REGULAR((3,)), dma((15,)), dma((2, 2)), dma((2, 2)), dma((SIDE,)), dma((8,)), dma((4, SIDE)), dma((4, SIDE)),
            dma((2, SIDE)), dma((2, SIDE)), dma((2, SIDE)), dma((2, SIDE)),
        ],
        compiler_params=pltpu.CompilerParams(
            collective_id=0, has_side_effects=True, vmem_limit_bytes=60 * 2**20
        ),
    )(
        latent_start, noise_draws[0], time_embed, step_scale, noise_scale,
        w_in.transpose(2, 3, 4, 1, 0).reshape(27 * CH, FT), b_in, gain_in, shift_in,
        w_mid.transpose(2, 3, 4, 0, 1).reshape(27 * FT, FT), b_mid, gain_mid, shift_mid,
        w_out.transpose(2, 3, 4, 0, 1).reshape(27 * CH, FT), b_out,
    )
    return out[None]


def solution(mesh):
    in_specs = (
        P(None, "gz", None, None), P("tm", None, "gz", None, None), P("tm", None), P("tm"), P("tm"),
        P(), P(), P(), P(), P(), P(), P(), P(), P(), P(),
    )
    out_specs = P("tm", None, "gz", None, None)
    return jax.shard_map(shards, mesh=mesh, in_specs=in_specs, out_specs=out_specs, check_vma=False)
```

```python
import functools

import jax
import jax.numpy as jnp
from jax import lax
from jax.experimental import pallas as pl
from jax.experimental.pallas import tpu as pltpu
from jax.sharding import PartitionSpec as P

MESH = pl.DeviceIdType.MESH
F32, BF16 = jnp.float32, jnp.bfloat16
CH, FT, GR = 8, 32, 8
NY, NX, NZ = 8, 128, 4
SIDE = 16
HALO = 3
CELLS = (FT // GR) * NZ * NY * NX

GZ_ORDER = (12, 13, 4, 5, 8, 9, 14, 15, 10, 11, 2, 3, 6, 7, 1)
HALF = 8
HALF_ORDER = (7, 5, 6, 3, 4, 1, 2)


def flip(place, bits):
    for bit in (1, 2, 4, 8):
        if bits & bit:
            place = place + bit - 2 * bit * lax.rem(lax.div(place, bit), 2)
    return place


def unfold(count):
    row = lax.broadcasted_iota(jnp.int32, (count, 8 * count), 0)
    lane = lax.broadcasted_iota(jnp.int32, (count, 8 * count), 1)
    return (lax.div(lane, 8) == row).astype(F32).astype(BF16)


def tap_masks(lanes):
    y = lax.broadcasted_iota(jnp.int32, (8, lanes), 0)
    yin = lax.rem(lax.broadcasted_iota(jnp.int32, (8, lanes), 1), 8)
    return [yin == lax.rem(y + b + 7, 8) for b in range(3)]


def circulant(rows, masks):
    n, lanes = rows[0].shape
    out = jnp.zeros((n, 8, lanes), F32)
    for row, mask in zip(rows, masks):
        full = jnp.broadcast_to(row[:, None, :], (n, 8, lanes))
        out = jnp.where(jnp.broadcast_to(mask[None], (n, 8, lanes)), full, out)
    return out.reshape(8 * n, lanes)


def kernel(
    lat_hbm, noise_hbm, emb_hbm, step_hbm, nsc_hbm, win_hbm, bin_hbm, gin_hbm, sin_hbm,
    wmid_hbm, bmid_hbm, gmid_hbm, smid_hbm, wout_hbm, bout_hbm,
    out_ref,
    lat_ref, noise_ref, win_ref, wmid_ref, wout_ref, emb_ref, step_ref, nsc_ref,
    bin_ref, gin_ref, sin_ref, bmid_ref, gmid_ref, smid_ref, bout_ref,
    vext, shift_in, lifted, act, summed, actb, a_in, a_mid, a_out, x_mid, splat, splat_out, drift,
    stat, recv, send1, lat_chunk, chunk_a, chunk_b, half_sum, earlier_sum,
    relay_sem, load_sem, halo_ss, halo_rs, edge_ss, edge_rs, stat_ss, stat_rs, p1_ss, p1_rs, p2_ss, p2_rs, sum_ss, sum_rs,
):
    k = lax.axis_index("tm")
    g = lax.axis_index("gz")
    up, down = lax.rem(g + 1, SIDE), lax.rem(g + SIDE - 1, SIDE)
    gz_peers = [flip(g, bits) for bits in GZ_ORDER]
    tm_peers = [flip(k, bits) for bits in HALF_ORDER]
    late, place = lax.div(k, HALF), lax.rem(k, HALF)
    twin = flip(k, HALF)
    my_z, my_p = lax.div(place, 2), lax.rem(place, 2)
    pending = []

    barrier = pltpu.get_barrier_semaphore()
    beside, across = [flip(k, 2), flip(k, 4)], [flip(k, 1)]
    for peer in beside + across:
        pl.semaphore_signal(barrier, inc=1, device_id={"tm": peer}, device_id_type=MESH)
    for peer in gz_peers:
        pl.semaphore_signal(barrier, inc=1, device_id={"gz": peer}, device_id_type=MESH)

    @pl.when(late == 0)
    def _():
        pl.semaphore_signal(barrier, inc=1, device_id={"tm": twin}, device_id_type=MESH)

    loads = []
    for src, dst in (
        (lat_hbm, lat_ref), (wmid_hbm, wmid_ref), (wout_hbm, wout_ref), (win_hbm, win_ref), (emb_hbm, emb_ref),
        (bin_hbm, bin_ref), (gin_hbm, gin_ref), (sin_hbm, sin_ref), (bmid_hbm, bmid_ref), (gmid_hbm, gmid_ref),
        (smid_hbm, smid_ref), (bout_hbm, bout_ref), (step_hbm, step_ref), (nsc_hbm, nsc_ref), (noise_hbm, noise_ref),
    ):
        copy = pltpu.make_async_copy(src, dst, load_sem.at[len(loads)])
        copy.start()
        loads.append(copy)

    loads[0].wait()
    for z in range(NZ):
        plane = lat_ref[:, z].reshape(CH * NY, NX)
        vext[0, HALO + z] = plane.reshape(4, 16, NX).astype(BF16)
        lat_chunk[2 * z : 2 * z + 2] = plane.reshape(2, 4, NY, NX)

    pl.semaphore_wait(barrier, len(GZ_ORDER) + len(beside + across) + late)

    def relay(turn, peers):
        for peer in peers:
            pl.semaphore_signal(relay_sem.at[turn], inc=1, device_id={"tm": peer}, device_id_type=MESH)

    relay(0, beside)

    @pl.when(late == 1)
    def _():
        relay(2, [twin])

    @pl.when(late == 0)
    def _():
        earlier_sum[...] = jnp.zeros_like(earlier_sum)

    def send(src, dst, ss, rs, device):
        copy = pltpu.make_async_remote_copy(
            src_ref=src, dst_ref=dst, send_sem=ss, recv_sem=rs, device_id=device, device_id_type=MESH
        )
        copy.start()
        pending.append(copy)
        return copy

    def settle(copies):
        fresh = {id(copy) for copy in copies}
        for copy in pending:
            if id(copy) not in fresh:
                copy.wait_send()
        pending[:] = copies
        for copy in copies:
            copy.wait_recv()

    halo = [
        send(vext.at[0, pl.ds(NZ, HALO)], vext.at[0, pl.ds(0, HALO)],
             halo_ss.at[0, 0], halo_rs.at[0, 0], {"gz": up}),
        send(vext.at[0, pl.ds(HALO, HALO)], vext.at[0, pl.ds(HALO + NZ, HALO)],
             halo_ss.at[0, 1], halo_rs.at[0, 1], {"gz": down}),
    ]

    def load_mid():
        loads[1].wait()
        x_mid[...] = jnp.dot(wmid_ref[...], unfold(FT), preferred_element_type=F32)
        masks = tap_masks(256)
        for a in range(3):
            for block in range(12):
                first = a * 288 + 8 * block
                rows = [x_mid[first + 96 * b : first + 96 * b + 8, :] for b in range(3)]
                a_mid[64 * block : 64 * block + 64, 256 * a : 256 * a + 256] = circulant(rows, masks).astype(BF16)

    def load_out():
        loads[2].wait()
        masks = tap_masks(256)
        x_out = jnp.dot(wout_ref[...], unfold(FT), preferred_element_type=F32)
        for a in range(3):
            rows = [x_out[(a * 3 + b) * 24 : (a * 3 + b) * 24 + 24] for b in range(3)]
            a_out[:, 256 * a : 256 * a + 256] = circulant(rows, masks).astype(BF16)

    loads[3].wait()
    masks = tap_masks(576)
    rows = []
    for b in range(3):
        w_b = jnp.concatenate([win_ref[(a * 3 + b) * 24 : (a * 3 + b) * 24 + 24, :].astype(F32) for a in range(3)], axis=0)
        rows.append(jnp.dot(w_b.T.astype(BF16), unfold(72), preferred_element_type=F32))
    for block in range(4):
        part = [row[8 * block : 8 * block + 8] for row in rows]
        a_in[64 * block : 64 * block + 64, :] = circulant(part, masks).astype(BF16)

    for copy in loads[4:]:
        copy.wait()

    def spread(o, carry):
        at = pl.ds(pl.multiple_of(o * 8, 8), 8)
        for i, value in enumerate((
            bin_ref[o] + emb_ref[0, o], 0.5 * gin_ref[o], 0.5 * sin_ref[o],
            bmid_ref[o], 0.5 * gmid_ref[o], 0.5 * smid_ref[o],
        )):
            splat[i, at, :] = jnp.full((8, NX), value, F32)
        return carry

    lax.fori_loop(0, FT, spread, 0)
    for o in range(CH):
        splat_out[8 * o : 8 * o + 8, :] = jnp.full((8, NX), bout_ref[o], F32)
    step, noise_scale = step_ref[0], nsc_ref[0]

    def lanes(first, count=1):
        return slice(NX * first, NX * (first + count))

    sub = lax.broadcasted_iota(jnp.int32, (8, NX), 0)
    low = lax.broadcasted_iota(jnp.int32, (8, NX), 1) < NX // 2

    def lane_sums(groups):
        rows = jnp.concatenate([jnp.sum(t, axis=0, keepdims=True) for t in groups], axis=0)
        return jnp.broadcast_to(jnp.sum(rows, axis=1, keepdims=True), (8, NX))

    def fold(ref, planes, centre=None):
        plain, squares = [], []
        for gr in range(GR):
            tiles = []
            for q in planes:
                for c in range(4):
                    tile = ref[32 * gr + 8 * c : 32 * gr + 8 * c + 8, lanes(q)]
                    tiles.append(tile if centre is None else tile - jnp.broadcast_to(centre[gr : gr + 1], (8, NX)))
            plain.append(functools.reduce(lambda x, y: x + y, tiles))
            if centre is not None:
                squares.append(functools.reduce(lambda x, y: x + y, [t * t for t in tiles]))
        return plain, squares

    def centre_of(ref, planes):
        return lane_sums(fold(ref, planes)[0]) * (1.0 / (len(planes) * 4 * NY * NX))

    def announce(ref, inner, outer, centre, turn):
        plain, squares = fold(ref, inner, centre)
        plain2, squares2 = fold(ref, outer, centre)
        first = lane_sums([x + y for x, y in zip(plain, plain2)])
        second = lane_sums([x + y for x, y in zip(squares, squares2)])
        off = first * (1.0 / CELLS)
        tile = jnp.where(low, centre + off, second - first * off)
        stat[turn] = tile
        recv[turn, g] = tile
        return [
            send(stat.at[turn], recv.at[turn, g], stat_ss.at[turn, i], stat_rs.at[turn, i], {"gz": peer})
            for i, peer in enumerate(gz_peers)
        ]

    def gathered(copies, turn):
        settle(copies)
        every = recv[turn]
        total = jnp.sum(every, axis=0)
        mean = total * (1.0 / SIDE)
        off = every - mean[None]
        spread_of = jnp.sum(off * off, axis=0)
        var = (pltpu.roll(total, NX // 2, 1) + spread_of * CELLS) * (1.0 / (CELLS * SIDE))
        inv = lax.rsqrt(var + 1e-05)
        return jnp.where(low, mean, pltpu.roll(mean, NX // 2, 1)), jnp.where(low, inv, pltpu.roll(inv, NX // 2, 1))

    def activate(src, dst, planes, mean, inv, gain, shift):
        for gr in range(GR):
            at = slice(32 * gr, 32 * gr + 32)
            m = jnp.broadcast_to(mean[gr : gr + 1], (32, NX))
            f = jnp.broadcast_to(inv[gr : gr + 1], (32, NX)) * splat[gain, at, :]
            s = splat[shift, at, :]
            for q in planes:
                half = (src[at, lanes(q)] - m) * f + s
                dst[at, lanes(q)] = (half + half * jnp.tanh(half)).astype(BF16)

    def stack(src, planes):
        return jnp.concatenate([jnp.concatenate([src[:, lanes(q + a)] for q in planes], axis=1) for a in range(3)], axis=0)

    def turned(sweep, planes):
        for e in planes:
            plane = vext[sweep, e].reshape(CH * NY, NX)
            wide = plane.astype(F32)
            shift_in[0:64, lanes(e)] = pltpu.roll(wide, 1, 1).astype(BF16)
            shift_in[64:128, lanes(e)] = plane
            shift_in[128:192, lanes(e)] = pltpu.roll(wide, NX - 1, 1).astype(BF16)

    def lift(planes):
        out = jnp.dot(a_in[...], stack(shift_in, planes), preferred_element_type=F32)
        for i, q in enumerate(planes):
            lifted[:, lanes(q)] = out[:, lanes(i)] + splat[0]

    def middle(planes):
        rhs = stack(act, planes)
        taps = jnp.dot(a_mid[...], rhs, preferred_element_type=F32)
        for i, r in enumerate(planes):
            summed[:, lanes(r)] = (
                pltpu.roll(taps[0:256, lanes(i)], 1, 1) + taps[256:512, lanes(i)]
                + pltpu.roll(taps[512:768, lanes(i)], NX - 1, 1) + splat[3] + lifted[:, lanes(r + 1)]
            )

    for sweep in range(2):
        if sweep == 0:
            for z in range(NZ):
                draws = noise_ref[:, z].astype(F32).reshape(CH * NY, NX)
                drift[z] = step * splat_out[...] + noise_scale * draws
            turned(sweep, (3, 4, 5, 6))
            lift((3, 4))
            centre = centre_of(lifted, (3, 4))
            settle(halo)
            turned(sweep, (2, 7))
            lift((2, 5))
            copies = announce(lifted, (3, 4), (2, 5), centre, 0)
            pl.semaphore_wait(relay_sem.at[0], 2)
            relay(1, across)
            turned(sweep, (0, 1, 8, 9))
            lift((0, 1, 6, 7))
            load_mid()
        else:
            halo = [
                send(vext.at[1, pl.ds(NZ, 2)], vext.at[1, pl.ds(0, 2)],
                     halo_ss.at[1, 0], halo_rs.at[1, 0], {"gz": up}),
                send(vext.at[1, pl.ds(NZ, 2)], vext.at[1, pl.ds(HALO + NZ + 1, 2)],
                     halo_ss.at[1, 1], halo_rs.at[1, 1], {"gz": down}),
            ]
            turned(sweep, (2, 3, 4, 5, 6, 7))
            lift((2, 3, 4, 5))
            centre = centre_of(lifted, (3, 4))
            copies = announce(lifted, (3, 4), (2, 5), centre, 2)
            for copy in halo:
                copy.wait_recv()
            turned(sweep, (0, 1, 8, 9))
            lift((0, 1, 6, 7))
        mean, inv = gathered(copies, 2 * sweep)
        if sweep == 0:
            pl.semaphore_wait(relay_sem.at[1], 1)

        activate(lifted, act, (1, 2, 3, 4, 5, 6), mean, inv, 1, 2)
        middle((2, 3))
        centre = centre_of(summed, (2, 3))
        middle((1, 4))
        copies = announce(summed, (2, 3), (1, 4), centre, 2 * sweep + 1)
        activate(lifted, act, (0, 7), mean, inv, 1, 2)
        middle((0, 5))
        if sweep == 0:
            load_out()
        mean, inv = gathered(copies, 2 * sweep + 1)

        activate(summed, actb, range(6), mean, inv, 4, 5)
        taps = jnp.dot(a_out[...], stack(actb, range(NZ)), preferred_element_type=F32)
        for z in range(NZ):
            predicted = (
                pltpu.roll(taps[0:64, lanes(z)], 1, 1) + taps[64:128, lanes(z)]
                + pltpu.roll(taps[128:192, lanes(z)], NX - 1, 1)
            )
            send1[sweep, 2 * z : 2 * z + 2] = (step * predicted + drift[z]).reshape(2, 4, NY, NX)

        chunk_a[sweep, place] = send1[sweep, place]
        copies = [
            send(send1.at[sweep, lax.rem(peer, HALF)], chunk_a.at[sweep, place],
                 p1_ss.at[sweep, i], p1_rs.at[sweep, i], {"tm": peer})
            for i, peer in enumerate(tm_peers)
        ]
        settle(copies)

        def onward():
            return pltpu.make_async_remote_copy(
                src_ref=half_sum.at[sweep], dst_ref=earlier_sum.at[sweep], send_sem=sum_ss.at[sweep],
                recv_sem=sum_rs.at[sweep], device_id={"tm": twin}, device_id_type=MESH,
            )

        @pl.when(late == 0)
        def _():
            half_sum[sweep] = jnp.sum(chunk_a[sweep], axis=0)
            if sweep == 0:
                pl.semaphore_wait(relay_sem.at[2], 1)
            onward().start()

        @pl.when(late == 1)
        def _():
            onward().wait_recv()

        state = lat_chunk[place] + earlier_sum[sweep]
        for s in range(HALF):
            if sweep == 0:
                chunk_b[s] = state.reshape(2, 16, NX).astype(BF16)
            state = state + chunk_a[sweep, s]
            if sweep == 1:
                send1[2, s] = state
        copies = []
        if sweep == 0:
            face = (my_z == 0) | (my_z == NZ - 1)
            first = my_z == 0
            other, plane = jnp.where(first, down, up), jnp.where(first, HALO + NZ, HALO - 1)
            edge = jnp.where(first, 2, 0) + my_p

            def edge_copy(i, peer):
                return pltpu.make_async_remote_copy(
                    src_ref=chunk_b.at[lax.rem(peer, HALF)], dst_ref=vext.at[1, plane, pl.ds(2 * my_p, 2)],
                    send_sem=edge_ss.at[i], recv_sem=edge_rs.at[edge],
                    device_id={"tm": peer, "gz": other}, device_id_type=MESH,
                )

            @pl.when(face)
            def _():
                for i, peer in enumerate(tm_peers + [k]):
                    edge_copy(i, peer).start()

        for i, peer in enumerate(tm_peers):
            if sweep == 0:
                src, dst = chunk_b.at[lax.rem(peer, HALF)], vext.at[1, HALO + my_z, pl.ds(2 * my_p, 2)]
            else:
                src, dst = send1.at[2, lax.rem(peer, HALF)], out_ref.at[pl.ds(4 * my_p, 4), my_z]
            copies.append(send(src, dst, p2_ss.at[sweep, i], p2_rs.at[sweep, i], {"tm": peer}))
        if sweep == 0:
            vext[1, HALO + my_z, pl.ds(2 * my_p, 2)] = chunk_b[place]
        else:
            out_ref[pl.ds(4 * my_p, 4), my_z] = send1[2, place]
        settle(copies)
        if sweep == 0:
            for i in range(4):
                pltpu.make_async_remote_copy(
                    src_ref=chunk_b.at[0],
                    dst_ref=vext.at[1, HALO + NZ if i >= 2 else HALO - 1, pl.ds(2 * (i % 2), 2)],
                    send_sem=edge_ss.at[0], recv_sem=edge_rs.at[i], device_id={"gz": up}, device_id_type=MESH,
                ).wait_recv()

            @pl.when(face)
            def _():
                for i, peer in enumerate(tm_peers + [k]):
                    edge_copy(i, peer).wait_send()

        @pl.when(late == 0)
        def _():
            onward().wait_send()

    for copy in pending:
        copy.wait_send()


def shards(
    latent_start, noise_draws, time_embed, step_scale, noise_scale, w_in, b_in, gain_in, shift_in,
    w_mid, b_mid, gain_mid, shift_mid, w_out, b_out,
):
    vmem = pl.BlockSpec(memory_space=pltpu.VMEM)
    params = [pltpu.SMEM((FT,), F32)] * 6
    dma = pltpu.SemaphoreType.DMA
    out = pl.pallas_call(
        kernel,
        out_shape=pltpu.VMEM((CH, NZ, NY, NX), F32),
        in_specs=[pl.BlockSpec(memory_space=pl.ANY)] * 15,
        out_specs=vmem,
        scratch_shapes=[
            pltpu.VMEM((CH, NZ, NY, NX), F32), pltpu.VMEM((CH, NZ, NY, NX), BF16),
            pltpu.VMEM((27 * CH, FT), BF16), pltpu.VMEM((27 * FT, FT), BF16), pltpu.VMEM((27 * CH, FT), BF16),
            pltpu.SMEM((1, FT), F32), pltpu.SMEM((1,), F32), pltpu.SMEM((1,), F32), *params, pltpu.SMEM((CH,), F32),
            pltpu.VMEM((2, NZ + 2 * HALO, 4, 16, NX), BF16),
            pltpu.VMEM((192, (NZ + 2 * HALO) * NX), BF16),
            pltpu.VMEM((256, 8 * NX), F32),
            pltpu.VMEM((256, 8 * NX), BF16),
            pltpu.VMEM((256, 6 * NX), F32),
            pltpu.VMEM((256, 6 * NX), BF16),
            pltpu.VMEM((256, 576), BF16),
            pltpu.VMEM((768, 768), BF16),
            pltpu.VMEM((192, 768), BF16),
            pltpu.VMEM((864, 256), F32),
            pltpu.VMEM((6, 256, NX), F32),
            pltpu.VMEM((64, NX), F32),
            pltpu.VMEM((NZ, 64, NX), F32),
            pltpu.VMEM((4, 8, NX), F32),
            pltpu.VMEM((4, SIDE, 8, NX), F32),
            pltpu.VMEM((3, HALF, 4, NY, NX), F32),
            pltpu.VMEM((HALF, 4, NY, NX), F32),
            pltpu.VMEM((2, HALF, 4, NY, NX), F32),
            pltpu.VMEM((HALF, 2, 16, NX), BF16),
            pltpu.VMEM((2, 4, NY, NX), F32),
            pltpu.VMEM((2, 4, NY, NX), F32),
            pltpu.SemaphoreType.REGULAR((3,)), dma((15,)), dma((2, 2)), dma((2, 2)), dma((HALF,)), dma((4,)), dma((4, SIDE)), dma((4, SIDE)),
            dma((2, HALF)), dma((2, HALF)), dma((2, HALF)), dma((2, HALF)), dma((2,)), dma((2,)),
        ],
        compiler_params=pltpu.CompilerParams(
            collective_id=0, has_side_effects=True, vmem_limit_bytes=60 * 2**20
        ),
    )(
        latent_start, noise_draws[0], time_embed, step_scale, noise_scale,
        w_in.transpose(2, 3, 4, 1, 0).reshape(27 * CH, FT), b_in, gain_in, shift_in,
        w_mid.transpose(2, 3, 4, 0, 1).reshape(27 * FT, FT), b_mid, gain_mid, shift_mid,
        w_out.transpose(2, 3, 4, 0, 1).reshape(27 * CH, FT), b_out,
    )
    return out[None]


def solution(mesh):
    in_specs = (
        P(None, "gz", None, None), P("tm", None, "gz", None, None), P("tm", None), P("tm"), P("tm"),
        P(), P(), P(), P(), P(), P(), P(), P(), P(), P(),
    )
    out_specs = P("tm", None, "gz", None, None)
    return jax.shard_map(shards, mesh=mesh, in_specs=in_specs, out_specs=out_specs, check_vma=False)
```

```python
import functools

import jax
import jax.numpy as jnp
from jax import lax
from jax.experimental import pallas as pl
from jax.experimental.pallas import tpu as pltpu
from jax.sharding import PartitionSpec as P

MESH = pl.DeviceIdType.MESH
F32, BF16 = jnp.float32, jnp.bfloat16
CH, FT, GR = 8, 32, 8
NY, NX, NZ = 8, 128, 4
SIDE = 16
HALO = 3
CELLS = (FT // GR) * NZ * NY * NX

GZ_ORDER = (12, 13, 4, 5, 8, 9, 14, 15, 10, 11, 2, 3, 6, 7, 1)
HALF = 8
HALF_ORDER = (7, 5, 6, 3, 4, 1, 2)


def flip(place, bits):
    for bit in (1, 2, 4, 8):
        if bits & bit:
            place = place + bit - 2 * bit * lax.rem(lax.div(place, bit), 2)
    return place


def unfold(count):
    row = lax.broadcasted_iota(jnp.int32, (count, 8 * count), 0)
    lane = lax.broadcasted_iota(jnp.int32, (count, 8 * count), 1)
    return (lax.div(lane, 8) == row).astype(F32).astype(BF16)


def tap_masks(lanes):
    y = lax.broadcasted_iota(jnp.int32, (8, lanes), 0)
    yin = lax.rem(lax.broadcasted_iota(jnp.int32, (8, lanes), 1), 8)
    return [yin == lax.rem(y + b + 7, 8) for b in range(3)]


def circulant(rows, masks):
    n, lanes = rows[0].shape
    out = jnp.zeros((n, 8, lanes), F32)
    for row, mask in zip(rows, masks):
        full = jnp.broadcast_to(row[:, None, :], (n, 8, lanes))
        out = jnp.where(jnp.broadcast_to(mask[None], (n, 8, lanes)), full, out)
    return out.reshape(8 * n, lanes)


def kernel(
    lat_hbm, noise_hbm, emb_hbm, step_hbm, nsc_hbm, win_hbm, bin_hbm, gin_hbm, sin_hbm,
    wmid_hbm, bmid_hbm, gmid_hbm, smid_hbm, wout_hbm, bout_hbm,
    out_ref,
    lat_ref, noise_ref, win_ref, wmid_ref, wout_ref, emb_ref, step_ref, nsc_ref,
    bin_ref, gin_ref, sin_ref, bmid_ref, gmid_ref, smid_ref, bout_ref,
    vext, shift_in, lifted, act, summed, actb, a_in, a_mid, a_out, x_mid, splat, splat_out, drift,
    stat, recv, send1, lat_chunk, chunk_a, chunk_b, half_sum, earlier_sum,
    relay_sem, load_sem, halo_ss, halo_rs, edge_ss, edge_rs, stat_ss, stat_rs, p1_ss, p1_rs, p2_ss, p2_rs, sum_ss, sum_rs,
):
    k = lax.axis_index("tm")
    g = lax.axis_index("gz")
    up, down = lax.rem(g + 1, SIDE), lax.rem(g + SIDE - 1, SIDE)
    gz_peers = [flip(g, bits) for bits in GZ_ORDER]
    tm_peers = [flip(k, bits) for bits in HALF_ORDER]
    late, place = lax.div(k, HALF), lax.rem(k, HALF)
    twin = flip(k, HALF + 4)

    def owned(device):
        at = lax.rem(device, HALF)
        return at + late * (4 - 8 * lax.div(at, 4))

    mine = owned(k)
    my_z, my_p = lax.div(mine, 2), lax.rem(mine, 2)
    pending = []

    barrier = pltpu.get_barrier_semaphore()
    beside, across = [flip(k, 2), flip(k, 4)], [flip(k, 1)]
    for peer in beside + across:
        pl.semaphore_signal(barrier, inc=1, device_id={"tm": peer}, device_id_type=MESH)
    for peer in gz_peers[2:]:
        pl.semaphore_signal(barrier, inc=1, device_id={"gz": peer}, device_id_type=MESH)

    @pl.when(late == 0)
    def _():
        pl.semaphore_signal(barrier, inc=1, device_id={"tm": twin}, device_id_type=MESH)

    loads = []
    for src, dst in (
        (lat_hbm, lat_ref), (wmid_hbm, wmid_ref), (wout_hbm, wout_ref), (win_hbm, win_ref), (emb_hbm, emb_ref),
        (bin_hbm, bin_ref), (gin_hbm, gin_ref), (sin_hbm, sin_ref), (bmid_hbm, bmid_ref), (gmid_hbm, gmid_ref),
        (smid_hbm, smid_ref), (bout_hbm, bout_ref), (step_hbm, step_ref), (nsc_hbm, nsc_ref), (noise_hbm, noise_ref),
    ):
        copy = pltpu.make_async_copy(src, dst, load_sem.at[len(loads)])
        copy.start()
        loads.append(copy)

    loads[0].wait()
    for z in range(NZ):
        plane = lat_ref[:, z].reshape(CH * NY, NX)
        vext[0, HALO + z] = plane.reshape(4, 16, NX).astype(BF16)
        lat_chunk[2 * z : 2 * z + 2] = plane.reshape(2, 4, NY, NX)

    pl.semaphore_wait(barrier, len(GZ_ORDER) - 2 + len(beside + across) + late)

    def relay(turn, peers):
        for peer in peers:
            pl.semaphore_signal(relay_sem.at[turn], inc=1, device_id={"tm": peer}, device_id_type=MESH)

    relay(0, beside)
    pl.semaphore_signal(relay_sem.at[3], inc=1, device_id={"gz": flip(g, 4)}, device_id_type=MESH)

    @pl.when(late == 1)
    def _():
        relay(2, [twin])

    @pl.when(late == 0)
    def _():
        earlier_sum[...] = jnp.zeros_like(earlier_sum)

    def send(src, dst, ss, rs, device):
        copy = pltpu.make_async_remote_copy(
            src_ref=src, dst_ref=dst, send_sem=ss, recv_sem=rs, device_id=device, device_id_type=MESH
        )
        copy.start()
        pending.append(copy)
        return copy

    def settle(copies):
        fresh = {id(copy) for copy in copies}
        for copy in pending:
            if id(copy) not in fresh:
                copy.wait_send()
        pending[:] = copies
        for copy in copies:
            copy.wait_recv()

    halo = [
        send(vext.at[0, pl.ds(NZ, HALO)], vext.at[0, pl.ds(0, HALO)],
             halo_ss.at[0, 0], halo_rs.at[0, 0], {"gz": up}),
        send(vext.at[0, pl.ds(HALO, HALO)], vext.at[0, pl.ds(HALO + NZ, HALO)],
             halo_ss.at[0, 1], halo_rs.at[0, 1], {"gz": down}),
    ]

    def load_mid():
        loads[1].wait()
        x_mid[...] = jnp.dot(wmid_ref[...], unfold(FT), preferred_element_type=F32)
        masks = tap_masks(256)
        for a in range(3):
            for block in range(12):
                first = a * 288 + 8 * block
                rows = [x_mid[first + 96 * b : first + 96 * b + 8, :] for b in range(3)]
                a_mid[64 * block : 64 * block + 64, 256 * a : 256 * a + 256] = circulant(rows, masks).astype(BF16)

    def load_out():
        loads[2].wait()
        masks = tap_masks(256)
        x_out = jnp.dot(wout_ref[...], unfold(FT), preferred_element_type=F32)
        for a in range(3):
            rows = [x_out[(a * 3 + b) * 24 : (a * 3 + b) * 24 + 24] for b in range(3)]
            a_out[:, 256 * a : 256 * a + 256] = circulant(rows, masks).astype(BF16)

    loads[3].wait()
    masks = tap_masks(576)
    rows = []
    for b in range(3):
        w_b = jnp.concatenate([win_ref[(a * 3 + b) * 24 : (a * 3 + b) * 24 + 24, :].astype(F32) for a in range(3)], axis=0)
        rows.append(jnp.dot(w_b.T.astype(BF16), unfold(72), preferred_element_type=F32))
    for block in range(4):
        part = [row[8 * block : 8 * block + 8] for row in rows]
        a_in[64 * block : 64 * block + 64, :] = circulant(part, masks).astype(BF16)

    for copy in loads[4:]:
        copy.wait()

    def spread(o, carry):
        at = pl.ds(pl.multiple_of(o * 8, 8), 8)
        for i, value in enumerate((
            bin_ref[o] + emb_ref[0, o], 0.5 * gin_ref[o], 0.5 * sin_ref[o],
            bmid_ref[o], 0.5 * gmid_ref[o], 0.5 * smid_ref[o],
        )):
            splat[i, at, :] = jnp.full((8, NX), value, F32)
        return carry

    lax.fori_loop(0, FT, spread, 0)
    for o in range(CH):
        splat_out[8 * o : 8 * o + 8, :] = jnp.full((8, NX), bout_ref[o], F32)
    step, noise_scale = step_ref[0], nsc_ref[0]

    def lanes(first, count=1):
        return slice(NX * first, NX * (first + count))

    sub = lax.broadcasted_iota(jnp.int32, (8, NX), 0)
    low = lax.broadcasted_iota(jnp.int32, (8, NX), 1) < NX // 2

    def lane_sums(groups):
        rows = jnp.concatenate([jnp.sum(t, axis=0, keepdims=True) for t in groups], axis=0)
        return jnp.broadcast_to(jnp.sum(rows, axis=1, keepdims=True), (8, NX))

    def fold(ref, planes, centre=None):
        plain, squares = [], []
        for gr in range(GR):
            tiles = []
            for q in planes:
                for c in range(4):
                    tile = ref[32 * gr + 8 * c : 32 * gr + 8 * c + 8, lanes(q)]
                    tiles.append(tile if centre is None else tile - jnp.broadcast_to(centre[gr : gr + 1], (8, NX)))
            plain.append(functools.reduce(lambda x, y: x + y, tiles))
            if centre is not None:
                squares.append(functools.reduce(lambda x, y: x + y, [t * t for t in tiles]))
        return plain, squares

    def centre_of(ref, planes):
        return lane_sums(fold(ref, planes)[0]) * (1.0 / (len(planes) * 4 * NY * NX))

    def announce(ref, inner, outer, centre, turn):
        plain, squares = fold(ref, inner, centre)
        plain2, squares2 = fold(ref, outer, centre)
        first = lane_sums([x + y for x, y in zip(plain, plain2)])
        second = lane_sums([x + y for x, y in zip(squares, squares2)])
        off = first * (1.0 / CELLS)
        tile = jnp.where(low, centre + off, second - first * off)
        stat[turn] = tile
        recv[turn, g] = tile
        return [
            send(stat.at[turn], recv.at[turn, g], stat_ss.at[turn, i], stat_rs.at[turn, i], {"gz": peer})
            for i, peer in enumerate(gz_peers)
        ]

    def gathered(copies, turn):
        settle(copies)
        every = recv[turn]
        total = jnp.sum(every, axis=0)
        mean = total * (1.0 / SIDE)
        off = every - mean[None]
        spread_of = jnp.sum(off * off, axis=0)
        var = (pltpu.roll(total, NX // 2, 1) + spread_of * CELLS) * (1.0 / (CELLS * SIDE))
        inv = lax.rsqrt(var + 1e-05)
        return jnp.where(low, mean, pltpu.roll(mean, NX // 2, 1)), jnp.where(low, inv, pltpu.roll(inv, NX // 2, 1))

    def activate(src, dst, planes, mean, inv, gain, shift):
        for gr in range(GR):
            at = slice(32 * gr, 32 * gr + 32)
            m = jnp.broadcast_to(mean[gr : gr + 1], (32, NX))
            f = jnp.broadcast_to(inv[gr : gr + 1], (32, NX)) * splat[gain, at, :]
            s = splat[shift, at, :]
            for q in planes:
                half = (src[at, lanes(q)] - m) * f + s
                dst[at, lanes(q)] = (half + half * jnp.tanh(half)).astype(BF16)

    def stack(src, planes):
        return jnp.concatenate([jnp.concatenate([src[:, lanes(q + a)] for q in planes], axis=1) for a in range(3)], axis=0)

    def turned(sweep, planes):
        for e in planes:
            plane = vext[sweep, e].reshape(CH * NY, NX)
            wide = plane.astype(F32)
            shift_in[0:64, lanes(e)] = pltpu.roll(wide, 1, 1).astype(BF16)
            shift_in[64:128, lanes(e)] = plane
            shift_in[128:192, lanes(e)] = pltpu.roll(wide, NX - 1, 1).astype(BF16)

    def lift(planes):
        out = jnp.dot(a_in[...], stack(shift_in, planes), preferred_element_type=F32)
        for i, q in enumerate(planes):
            lifted[:, lanes(q)] = out[:, lanes(i)] + splat[0]

    def middle(planes):
        rhs = stack(act, planes)
        taps = [jnp.dot(a_mid[256 * c : 256 * c + 256, :], rhs, preferred_element_type=F32) for c in range(3)]
        for i, r in enumerate(planes):
            summed[:, lanes(r)] = (
                pltpu.roll(taps[0][:, lanes(i)], 1, 1) + taps[1][:, lanes(i)]
                + pltpu.roll(taps[2][:, lanes(i)], NX - 1, 1) + splat[3] + lifted[:, lanes(r + 1)]
            )

    for sweep in range(2):
        if sweep == 0:
            for z in range(NZ):
                draws = noise_ref[:, z].astype(F32).reshape(CH * NY, NX)
                drift[z] = step * splat_out[...] + noise_scale * draws
            turned(sweep, (3, 4, 5, 6))
            lift((3, 4))
            centre = centre_of(lifted, (3, 4))
            settle(halo)
            turned(sweep, (2, 7))
            lift((2, 5))
            pl.semaphore_wait(relay_sem.at[3], 1)
            copies = announce(lifted, (3, 4), (2, 5), centre, 0)
            pl.semaphore_wait(relay_sem.at[0], 2)
            relay(1, across)
            turned(sweep, (0, 1, 8, 9))
            lift((0, 1, 6, 7))
            load_mid()
        else:
            halo = [
                send(vext.at[1, pl.ds(NZ, 2)], vext.at[1, pl.ds(0, 2)],
                     halo_ss.at[1, 0], halo_rs.at[1, 0], {"gz": up}),
                send(vext.at[1, pl.ds(NZ, 2)], vext.at[1, pl.ds(HALO + NZ + 1, 2)],
                     halo_ss.at[1, 1], halo_rs.at[1, 1], {"gz": down}),
            ]
            turned(sweep, (2, 3, 4, 5, 6, 7))
            lift((2, 3, 4, 5))
            centre = centre_of(lifted, (3, 4))
            copies = announce(lifted, (3, 4), (2, 5), centre, 2)
            for copy in halo:
                copy.wait_recv()
            turned(sweep, (0, 1, 8, 9))
            lift((0, 1, 6, 7))
        mean, inv = gathered(copies, 2 * sweep)
        if sweep == 0:
            pl.semaphore_wait(relay_sem.at[1], 1)

        activate(lifted, act, (1, 2, 3, 4, 5, 6), mean, inv, 1, 2)
        middle((2, 3))
        centre = centre_of(summed, (2, 3))
        middle((1, 4))
        copies = announce(summed, (2, 3), (1, 4), centre, 2 * sweep + 1)
        activate(lifted, act, (0, 7), mean, inv, 1, 2)
        middle((0, 5))
        if sweep == 0:
            load_out()
        mean, inv = gathered(copies, 2 * sweep + 1)

        activate(summed, actb, range(6), mean, inv, 4, 5)
        taps = jnp.dot(a_out[...], stack(actb, range(NZ)), preferred_element_type=F32)
        for z in range(NZ):
            predicted = (
                pltpu.roll(taps[0:64, lanes(z)], 1, 1) + taps[64:128, lanes(z)]
                + pltpu.roll(taps[128:192, lanes(z)], NX - 1, 1)
            )
            send1[sweep, 2 * z : 2 * z + 2] = (step * predicted + drift[z]).reshape(2, 4, NY, NX)

        chunk_a[sweep, place] = send1[sweep, mine]
        copies = [
            send(send1.at[sweep, owned(peer)], chunk_a.at[sweep, place],
                 p1_ss.at[sweep, i], p1_rs.at[sweep, i], {"tm": peer})
            for i, peer in enumerate(tm_peers)
        ]
        settle(copies)

        def onward():
            return pltpu.make_async_remote_copy(
                src_ref=half_sum.at[sweep], dst_ref=earlier_sum.at[sweep], send_sem=sum_ss.at[sweep],
                recv_sem=sum_rs.at[sweep], device_id={"tm": twin}, device_id_type=MESH,
            )

        @pl.when(late == 0)
        def _():
            half_sum[sweep] = jnp.sum(chunk_a[sweep], axis=0)
            if sweep == 0:
                pl.semaphore_wait(relay_sem.at[2], 1)
            onward().start()

        @pl.when(late == 1)
        def _():
            onward().wait_recv()

        state = lat_chunk[mine] + earlier_sum[sweep]
        for s in range(HALF):
            if sweep == 0:
                chunk_b[s] = state.reshape(2, 16, NX).astype(BF16)
            state = state + chunk_a[sweep, s]
            if sweep == 1:
                send1[2, s] = state
        copies = []
        if sweep == 0:
            face = (my_z == 0) | (my_z == NZ - 1)
            first = my_z == 0
            other, plane = jnp.where(first, down, up), jnp.where(first, HALO + NZ, HALO - 1)
            edge = jnp.where(first, 2, 0) + my_p

            def edge_copy(i, peer):
                return pltpu.make_async_remote_copy(
                    src_ref=chunk_b.at[lax.rem(peer, HALF)], dst_ref=vext.at[1, plane, pl.ds(2 * my_p, 2)],
                    send_sem=edge_ss.at[i], recv_sem=edge_rs.at[edge],
                    device_id={"tm": peer, "gz": other}, device_id_type=MESH,
                )

            @pl.when(face)
            def _():
                for i, peer in enumerate(tm_peers + [k]):
                    edge_copy(i, peer).start()

        for i, peer in enumerate(tm_peers):
            if sweep == 0:
                src, dst = chunk_b.at[lax.rem(peer, HALF)], vext.at[1, HALO + my_z, pl.ds(2 * my_p, 2)]
            else:
                src, dst = send1.at[2, lax.rem(peer, HALF)], out_ref.at[pl.ds(4 * my_p, 4), my_z]
            copies.append(send(src, dst, p2_ss.at[sweep, i], p2_rs.at[sweep, i], {"tm": peer}))
        if sweep == 0:
            vext[1, HALO + my_z, pl.ds(2 * my_p, 2)] = chunk_b[place]
        else:
            out_ref[pl.ds(4 * my_p, 4), my_z] = send1[2, place]
        settle(copies)
        if sweep == 0:
            for i in range(4):
                pltpu.make_async_remote_copy(
                    src_ref=chunk_b.at[0],
                    dst_ref=vext.at[1, HALO + NZ if i >= 2 else HALO - 1, pl.ds(2 * (i % 2), 2)],
                    send_sem=edge_ss.at[0], recv_sem=edge_rs.at[i], device_id={"gz": up}, device_id_type=MESH,
                ).wait_recv()

            @pl.when(face)
            def _():
                for i, peer in enumerate(tm_peers + [k]):
                    edge_copy(i, peer).wait_send()

        @pl.when(late == 0)
        def _():
            onward().wait_send()

    for copy in pending:
        copy.wait_send()


def shards(
    latent_start, noise_draws, time_embed, step_scale, noise_scale, w_in, b_in, gain_in, shift_in,
    w_mid, b_mid, gain_mid, shift_mid, w_out, b_out,
):
    vmem = pl.BlockSpec(memory_space=pltpu.VMEM)
    params = [pltpu.SMEM((FT,), F32)] * 6
    dma = pltpu.SemaphoreType.DMA
    out = pl.pallas_call(
        kernel,
        out_shape=pltpu.VMEM((CH, NZ, NY, NX), F32),
        in_specs=[pl.BlockSpec(memory_space=pl.ANY)] * 15,
        out_specs=vmem,
        scratch_shapes=[
            pltpu.VMEM((CH, NZ, NY, NX), F32), pltpu.VMEM((CH, NZ, NY, NX), BF16),
            pltpu.VMEM((27 * CH, FT), BF16), pltpu.VMEM((27 * FT, FT), BF16), pltpu.VMEM((27 * CH, FT), BF16),
            pltpu.SMEM((1, FT), F32), pltpu.SMEM((1,), F32), pltpu.SMEM((1,), F32), *params, pltpu.SMEM((CH,), F32),
            pltpu.VMEM((2, NZ + 2 * HALO, 4, 16, NX), BF16),
            pltpu.VMEM((192, (NZ + 2 * HALO) * NX), BF16),
            pltpu.VMEM((256, 8 * NX), F32),
            pltpu.VMEM((256, 8 * NX), BF16),
            pltpu.VMEM((256, 6 * NX), F32),
            pltpu.VMEM((256, 6 * NX), BF16),
            pltpu.VMEM((256, 576), BF16),
            pltpu.VMEM((768, 768), BF16),
            pltpu.VMEM((192, 768), BF16),
            pltpu.VMEM((864, 256), F32),
            pltpu.VMEM((6, 256, NX), F32),
            pltpu.VMEM((64, NX), F32),
            pltpu.VMEM((NZ, 64, NX), F32),
            pltpu.VMEM((4, 8, NX), F32),
            pltpu.VMEM((4, SIDE, 8, NX), F32),
            pltpu.VMEM((3, HALF, 4, NY, NX), F32),
            pltpu.VMEM((HALF, 4, NY, NX), F32),
            pltpu.VMEM((2, HALF, 4, NY, NX), F32),
            pltpu.VMEM((HALF, 2, 16, NX), BF16),
            pltpu.VMEM((2, 4, NY, NX), F32),
            pltpu.VMEM((2, 4, NY, NX), F32),
            pltpu.SemaphoreType.REGULAR((4,)), dma((15,)), dma((2, 2)), dma((2, 2)), dma((HALF,)), dma((4,)), dma((4, SIDE)), dma((4, SIDE)),
            dma((2, HALF)), dma((2, HALF)), dma((2, HALF)), dma((2, HALF)), dma((2,)), dma((2,)),
        ],
        compiler_params=pltpu.CompilerParams(
            collective_id=0, has_side_effects=True, vmem_limit_bytes=60 * 2**20
        ),
    )(
        latent_start, noise_draws[0], time_embed, step_scale, noise_scale,
        w_in.transpose(2, 3, 4, 1, 0).reshape(27 * CH, FT), b_in, gain_in, shift_in,
        w_mid.transpose(2, 3, 4, 0, 1).reshape(27 * FT, FT), b_mid, gain_mid, shift_mid,
        w_out.transpose(2, 3, 4, 0, 1).reshape(27 * CH, FT), b_out,
    )
    return out[None]


def solution(mesh):
    in_specs = (
        P(None, "gz", None, None), P("tm", None, "gz", None, None), P("tm", None), P("tm"), P("tm"),
        P(), P(), P(), P(), P(), P(), P(), P(), P(), P(),
    )
    out_specs = P("tm", None, "gz", None, None)
    return jax.shard_map(shards, mesh=mesh, in_specs=in_specs, out_specs=out_specs, check_vma=False)
```

```python
import functools

import jax
import jax.numpy as jnp
from jax import lax
from jax.experimental import pallas as pl
from jax.experimental.pallas import tpu as pltpu
from jax.sharding import PartitionSpec as P

MESH = pl.DeviceIdType.MESH
F32, BF16 = jnp.float32, jnp.bfloat16
CH, FT, GR = 8, 32, 8
NY, NX, NZ = 8, 128, 4
SIDE = 16
HALO = 3
CELLS = (FT // GR) * NZ * NY * NX

GZ_ORDER = (12, 13, 4, 5, 8, 9, 14, 15, 10, 11, 2, 3, 6, 7, 1)
HALF = 8
HALF_ORDER = (7, 5, 6, 3, 4, 1, 2)


def flip(place, bits):
    for bit in (1, 2, 4, 8):
        if bits & bit:
            place = place + bit - 2 * bit * lax.rem(lax.div(place, bit), 2)
    return place


def unfold(count):
    row = lax.broadcasted_iota(jnp.int32, (count, 8 * count), 0)
    lane = lax.broadcasted_iota(jnp.int32, (count, 8 * count), 1)
    return (lax.div(lane, 8) == row).astype(F32).astype(BF16)


def tap_masks(lanes):
    y = lax.broadcasted_iota(jnp.int32, (8, lanes), 0)
    yin = lax.rem(lax.broadcasted_iota(jnp.int32, (8, lanes), 1), 8)
    return [yin == lax.rem(y + b + 7, 8) for b in range(3)]


def circulant(rows, masks):
    n, lanes = rows[0].shape
    out = jnp.zeros((n, 8, lanes), F32)
    for row, mask in zip(rows, masks):
        full = jnp.broadcast_to(row[:, None, :], (n, 8, lanes))
        out = jnp.where(jnp.broadcast_to(mask[None], (n, 8, lanes)), full, out)
    return out.reshape(8 * n, lanes)


def kernel(
    lat_hbm, noise_hbm, emb_hbm, step_hbm, nsc_hbm, win_hbm, bin_hbm, gin_hbm, sin_hbm,
    wmid_hbm, bmid_hbm, gmid_hbm, smid_hbm, wout_hbm, bout_hbm,
    out_ref,
    lat_ref, noise_ref, win_ref, wmid_ref, wout_ref, emb_ref, step_ref, nsc_ref,
    bin_ref, gin_ref, sin_ref, bmid_ref, gmid_ref, smid_ref, bout_ref,
    vext, shift_in, lifted, act, summed, actb, a_in, a_mid, a_out, x_mid, splat, splat_out, drift,
    stat, recv, send1, lat_chunk, chunk_a, chunk_b, half_sum, earlier_sum,
    relay_sem, load_sem, halo_ss, halo_rs, edge_ss, edge_rs, stat_ss, stat_rs, p1_ss, p1_rs, p2_ss, p2_rs, sum_ss, sum_rs,
):
    k = lax.axis_index("tm")
    g = lax.axis_index("gz")
    up, down = lax.rem(g + 1, SIDE), lax.rem(g + SIDE - 1, SIDE)
    gz_peers = [flip(g, bits) for bits in GZ_ORDER]
    tm_peers = [flip(k, bits) for bits in HALF_ORDER]
    late, place = lax.div(k, HALF), lax.rem(k, HALF)
    twin = flip(k, HALF + 4)

    def owned(device):
        at = lax.rem(device, HALF)
        return at + late * (4 - 8 * lax.div(at, 4))

    mine = owned(k)
    my_z, my_p = lax.div(mine, 2), lax.rem(mine, 2)
    pending = []

    barrier = pltpu.get_barrier_semaphore()
    beside, across = [flip(k, 2), flip(k, 4)], [flip(k, 1)]
    for peer in beside + across:
        pl.semaphore_signal(barrier, inc=1, device_id={"tm": peer}, device_id_type=MESH)
    for peer in gz_peers[2:]:
        pl.semaphore_signal(barrier, inc=1, device_id={"gz": peer}, device_id_type=MESH)

    @pl.when(late == 0)
    def _():
        pl.semaphore_signal(barrier, inc=1, device_id={"tm": twin}, device_id_type=MESH)

    loads = []
    for src, dst in (
        (lat_hbm, lat_ref), (wmid_hbm, wmid_ref), (wout_hbm, wout_ref), (win_hbm, win_ref), (emb_hbm, emb_ref),
        (bin_hbm, bin_ref), (gin_hbm, gin_ref), (sin_hbm, sin_ref), (bmid_hbm, bmid_ref), (gmid_hbm, gmid_ref),
        (smid_hbm, smid_ref), (bout_hbm, bout_ref), (step_hbm, step_ref), (nsc_hbm, nsc_ref), (noise_hbm, noise_ref),
    ):
        copy = pltpu.make_async_copy(src, dst, load_sem.at[len(loads)])
        copy.start()
        loads.append(copy)

    loads[0].wait()
    for z in range(NZ):
        plane = lat_ref[:, z].reshape(CH * NY, NX)
        vext[0, HALO + z] = plane.reshape(4, 16, NX).astype(BF16)
        lat_chunk[2 * z : 2 * z + 2] = plane.reshape(2, 4, NY, NX)

    pl.semaphore_wait(barrier, len(GZ_ORDER) - 2 + len(beside + across) + late)

    def relay(turn, peers):
        for peer in peers:
            pl.semaphore_signal(relay_sem.at[turn], inc=1, device_id={"tm": peer}, device_id_type=MESH)

    relay(0, beside)
    pl.semaphore_signal(relay_sem.at[3], inc=1, device_id={"gz": flip(g, 4)}, device_id_type=MESH)

    @pl.when(late == 1)
    def _():
        relay(2, [twin])

    @pl.when(late == 0)
    def _():
        earlier_sum[...] = jnp.zeros_like(earlier_sum)

    def send(src, dst, ss, rs, device):
        copy = pltpu.make_async_remote_copy(
            src_ref=src, dst_ref=dst, send_sem=ss, recv_sem=rs, device_id=device, device_id_type=MESH
        )
        copy.start()
        pending.append(copy)
        return copy

    def settle(copies):
        fresh = {id(copy) for copy in copies}
        for copy in pending:
            if id(copy) not in fresh:
                copy.wait_send()
        pending[:] = copies
        for copy in copies:
            copy.wait_recv()

    halo = [
        send(vext.at[0, pl.ds(NZ, HALO)], vext.at[0, pl.ds(0, HALO)],
             halo_ss.at[0, 0], halo_rs.at[0, 0], {"gz": up}),
        send(vext.at[0, pl.ds(HALO, HALO)], vext.at[0, pl.ds(HALO + NZ, HALO)],
             halo_ss.at[0, 1], halo_rs.at[0, 1], {"gz": down}),
    ]

    def load_mid():
        loads[1].wait()
        x_mid[...] = jnp.dot(wmid_ref[...], unfold(FT), preferred_element_type=F32)
        masks = tap_masks(256)
        for a in range(3):
            for block in range(12):
                first = a * 288 + 8 * block
                rows = [x_mid[first + 96 * b : first + 96 * b + 8, :] for b in range(3)]
                a_mid[64 * block : 64 * block + 64, 256 * a : 256 * a + 256] = circulant(rows, masks).astype(BF16)

    def load_out():
        loads[2].wait()
        masks = tap_masks(256)
        x_out = jnp.dot(wout_ref[...], unfold(FT), preferred_element_type=F32)
        for a in range(3):
            rows = [x_out[(a * 3 + b) * 24 : (a * 3 + b) * 24 + 24] for b in range(3)]
            a_out[:, 256 * a : 256 * a + 256] = circulant(rows, masks).astype(BF16)

    loads[3].wait()
    masks = tap_masks(576)
    rows = []
    for b in range(3):
        w_b = jnp.concatenate([win_ref[(a * 3 + b) * 24 : (a * 3 + b) * 24 + 24, :].astype(F32) for a in range(3)], axis=0)
        rows.append(jnp.dot(w_b.T.astype(BF16), unfold(72), preferred_element_type=F32))
    for block in range(4):
        part = [row[8 * block : 8 * block + 8] for row in rows]
        a_in[64 * block : 64 * block + 64, :] = circulant(part, masks).astype(BF16)

    for copy in loads[4:]:
        copy.wait()

    def spread(o, carry):
        at = pl.ds(pl.multiple_of(o * 8, 8), 8)
        for i, value in enumerate((
            bin_ref[o] + emb_ref[0, o], 0.5 * gin_ref[o], 0.5 * sin_ref[o],
            bmid_ref[o], 0.5 * gmid_ref[o], 0.5 * smid_ref[o],
        )):
            splat[i, at, :] = jnp.full((8, NX), value, F32)
        return carry

    lax.fori_loop(0, FT, spread, 0)
    for o in range(CH):
        splat_out[8 * o : 8 * o + 8, :] = jnp.full((8, NX), bout_ref[o], F32)
    step, noise_scale = step_ref[0], nsc_ref[0]

    def lanes(first, count=1):
        return slice(NX * first, NX * (first + count))

    sub = lax.broadcasted_iota(jnp.int32, (8, NX), 0)
    lane = lax.broadcasted_iota(jnp.int32, (8, NX), 1)
    own_lane, first_lane = lax.rem(lane, GR) == sub, lane == sub

    def lane_sums(groups):
        rows = jnp.concatenate([jnp.sum(t, axis=0, keepdims=True) for t in groups], axis=0)
        return jnp.broadcast_to(jnp.sum(rows, axis=1, keepdims=True), (8, NX))

    def fold(ref, planes, centre=None):
        plain, squares = [], []
        for gr in range(GR):
            tiles = []
            for q in planes:
                for c in range(4):
                    tile = ref[32 * gr + 8 * c : 32 * gr + 8 * c + 8, lanes(q)]
                    tiles.append(tile if centre is None else tile - jnp.broadcast_to(centre[gr : gr + 1], (8, NX)))
            plain.append(functools.reduce(lambda x, y: x + y, tiles))
            if centre is not None:
                squares.append(functools.reduce(lambda x, y: x + y, [t * t for t in tiles]))
        return plain, squares

    def centre_of(ref, planes):
        return lane_sums(fold(ref, planes)[0]) * (1.0 / (len(planes) * 4 * NY * NX))

    def announce(ref, inner, outer, centre, turn):
        plain, squares = fold(ref, inner, centre)
        plain2, squares2 = fold(ref, outer, centre)
        first = lane_sums([x + y for x, y in zip(plain, plain2)])
        second = lane_sums([x + y for x, y in zip(squares, squares2)])
        off = first * (1.0 / CELLS)
        both = jnp.where(lax.rem(lane, 2 * GR) < GR, centre + off, second - first * off)
        row = jnp.sum(jnp.where(own_lane, both, 0.0), axis=0, keepdims=True)
        stat[turn] = row
        recv[turn, g] = row
        return [
            send(stat.at[turn], recv.at[turn, g], stat_ss.at[turn, i], stat_rs.at[turn, i], {"gz": peer})
            for i, peer in enumerate(gz_peers)
        ]

    def gathered(copies, turn):
        settle(copies)
        every = recv[turn]
        total = jnp.sum(every, axis=0)
        mean = total * (1.0 / SIDE)
        off = every - mean[None]
        spread_of = jnp.sum(off * off, axis=0)
        var = (pltpu.roll(total, NX - GR, 1) + spread_of * CELLS) * (1.0 / (CELLS * SIDE))

        def by_row(row):
            picked = jnp.where(first_lane, jnp.broadcast_to(row, (8, NX)), 0.0)
            return jnp.broadcast_to(jnp.sum(picked, axis=1, keepdims=True), (8, NX))

        return by_row(mean), by_row(lax.rsqrt(var + 1e-05))

    def activate(src, dst, planes, mean, inv, gain, shift):
        for gr in range(GR):
            at = slice(32 * gr, 32 * gr + 32)
            m = jnp.broadcast_to(mean[gr : gr + 1], (32, NX))
            f = jnp.broadcast_to(inv[gr : gr + 1], (32, NX)) * splat[gain, at, :]
            s = splat[shift, at, :]
            for q in planes:
                half = (src[at, lanes(q)] - m) * f + s
                dst[at, lanes(q)] = (half + half * jnp.tanh(half)).astype(BF16)

    def stack(src, planes):
        return jnp.concatenate([jnp.concatenate([src[:, lanes(q + a)] for q in planes], axis=1) for a in range(3)], axis=0)

    def turned(sweep, planes):
        for e in planes:
            plane = vext[sweep, e].reshape(CH * NY, NX)
            wide = plane.astype(F32)
            shift_in[0:64, lanes(e)] = pltpu.roll(wide, 1, 1).astype(BF16)
            shift_in[64:128, lanes(e)] = plane
            shift_in[128:192, lanes(e)] = pltpu.roll(wide, NX - 1, 1).astype(BF16)

    def lift(planes):
        out = jnp.dot(a_in[...], stack(shift_in, planes), preferred_element_type=F32)
        for i, q in enumerate(planes):
            lifted[:, lanes(q)] = out[:, lanes(i)] + splat[0]

    def middle(planes):
        rhs = stack(act, planes)
        taps = [jnp.dot(a_mid[256 * c : 256 * c + 256, :], rhs, preferred_element_type=F32) for c in range(3)]
        for i, r in enumerate(planes):
            summed[:, lanes(r)] = (
                pltpu.roll(taps[0][:, lanes(i)], 1, 1) + taps[1][:, lanes(i)]
                + pltpu.roll(taps[2][:, lanes(i)], NX - 1, 1) + splat[3] + lifted[:, lanes(r + 1)]
            )

    for sweep in range(2):
        if sweep == 0:
            for z in range(NZ):
                draws = noise_ref[:, z].astype(F32).reshape(CH * NY, NX)
                drift[z] = step * splat_out[...] + noise_scale * draws
            turned(sweep, (3, 4, 5, 6))
            lift((3, 4))
            centre = centre_of(lifted, (3, 4))
            settle(halo)
            turned(sweep, (2, 7))
            lift((2, 5))
            pl.semaphore_wait(relay_sem.at[3], 1)
            copies = announce(lifted, (3, 4), (2, 5), centre, 0)
            pl.semaphore_wait(relay_sem.at[0], 2)
            relay(1, across)
            turned(sweep, (0, 1, 8, 9))
            lift((0, 1, 6, 7))
            load_mid()
        else:
            halo = [
                send(vext.at[1, pl.ds(NZ, 2)], vext.at[1, pl.ds(0, 2)],
                     halo_ss.at[1, 0], halo_rs.at[1, 0], {"gz": up}),
                send(vext.at[1, pl.ds(NZ, 2)], vext.at[1, pl.ds(HALO + NZ + 1, 2)],
                     halo_ss.at[1, 1], halo_rs.at[1, 1], {"gz": down}),
            ]
            turned(sweep, (2, 3, 4, 5, 6, 7))
            lift((3, 4))
            centre = centre_of(lifted, (3, 4))
            lift((2, 5))
            copies = announce(lifted, (3, 4), (2, 5), centre, 2)
            for copy in halo:
                copy.wait_recv()
            turned(sweep, (0, 1, 8, 9))
            lift((0, 1, 6, 7))
        mean, inv = gathered(copies, 2 * sweep)
        if sweep == 0:
            pl.semaphore_wait(relay_sem.at[1], 1)

        activate(lifted, act, (1, 2, 3, 4, 5, 6), mean, inv, 1, 2)
        middle((2, 3))
        centre = centre_of(summed, (2, 3))
        middle((1, 4))
        copies = announce(summed, (2, 3), (1, 4), centre, 2 * sweep + 1)
        activate(lifted, act, (0, 7), mean, inv, 1, 2)
        middle((0, 5))
        if sweep == 0:
            load_out()
        mean, inv = gathered(copies, 2 * sweep + 1)

        activate(summed, actb, range(6), mean, inv, 4, 5)
        taps = jnp.dot(a_out[...], stack(actb, range(NZ)), preferred_element_type=F32)
        for z in range(NZ):
            predicted = (
                pltpu.roll(taps[0:64, lanes(z)], 1, 1) + taps[64:128, lanes(z)]
                + pltpu.roll(taps[128:192, lanes(z)], NX - 1, 1)
            )
            send1[sweep, 2 * z : 2 * z + 2] = (step * predicted + drift[z]).reshape(2, 4, NY, NX)

        chunk_a[sweep, place] = send1[sweep, mine]
        copies = [
            send(send1.at[sweep, owned(peer)], chunk_a.at[sweep, place],
                 p1_ss.at[sweep, i], p1_rs.at[sweep, i], {"tm": peer})
            for i, peer in enumerate(tm_peers)
        ]
        settle(copies)

        def onward():
            return pltpu.make_async_remote_copy(
                src_ref=half_sum.at[sweep], dst_ref=earlier_sum.at[sweep], send_sem=sum_ss.at[sweep],
                recv_sem=sum_rs.at[sweep], device_id={"tm": twin}, device_id_type=MESH,
            )

        @pl.when(late == 0)
        def _():
            half_sum[sweep] = jnp.sum(chunk_a[sweep], axis=0)
            if sweep == 0:
                pl.semaphore_wait(relay_sem.at[2], 1)
            onward().start()

        @pl.when(late == 1)
        def _():
            onward().wait_recv()

        state = lat_chunk[mine] + earlier_sum[sweep]
        for s in range(HALF):
            if sweep == 0:
                chunk_b[s] = state.reshape(2, 16, NX).astype(BF16)
            state = state + chunk_a[sweep, s]
            if sweep == 1:
                send1[2, s] = state
        copies = []
        if sweep == 0:
            face = (my_z == 0) | (my_z == NZ - 1)
            first = my_z == 0
            other, plane = jnp.where(first, down, up), jnp.where(first, HALO + NZ, HALO - 1)
            edge = jnp.where(first, 2, 0) + my_p

            def edge_copy(i, peer):
                return pltpu.make_async_remote_copy(
                    src_ref=chunk_b.at[lax.rem(peer, HALF)], dst_ref=vext.at[1, plane, pl.ds(2 * my_p, 2)],
                    send_sem=edge_ss.at[i], recv_sem=edge_rs.at[edge],
                    device_id={"tm": peer, "gz": other}, device_id_type=MESH,
                )

            @pl.when(face)
            def _():
                for i, peer in enumerate(tm_peers + [k]):
                    edge_copy(i, peer).start()

        for i, peer in enumerate(tm_peers):
            if sweep == 0:
                src, dst = chunk_b.at[lax.rem(peer, HALF)], vext.at[1, HALO + my_z, pl.ds(2 * my_p, 2)]
            else:
                src, dst = send1.at[2, lax.rem(peer, HALF)], out_ref.at[pl.ds(4 * my_p, 4), my_z]
            copies.append(send(src, dst, p2_ss.at[sweep, i], p2_rs.at[sweep, i], {"tm": peer}))
        if sweep == 0:
            vext[1, HALO + my_z, pl.ds(2 * my_p, 2)] = chunk_b[place]
        else:
            out_ref[pl.ds(4 * my_p, 4), my_z] = send1[2, place]
        settle(copies)
        if sweep == 0:
            for i in range(4):
                pltpu.make_async_remote_copy(
                    src_ref=chunk_b.at[0],
                    dst_ref=vext.at[1, HALO + NZ if i >= 2 else HALO - 1, pl.ds(2 * (i % 2), 2)],
                    send_sem=edge_ss.at[0], recv_sem=edge_rs.at[i], device_id={"gz": up}, device_id_type=MESH,
                ).wait_recv()

            @pl.when(face)
            def _():
                for i, peer in enumerate(tm_peers + [k]):
                    edge_copy(i, peer).wait_send()

        @pl.when(late == 0)
        def _():
            onward().wait_send()

    for copy in pending:
        copy.wait_send()


def shards(
    latent_start, noise_draws, time_embed, step_scale, noise_scale, w_in, b_in, gain_in, shift_in,
    w_mid, b_mid, gain_mid, shift_mid, w_out, b_out,
):
    vmem = pl.BlockSpec(memory_space=pltpu.VMEM)
    params = [pltpu.SMEM((FT,), F32)] * 6
    dma = pltpu.SemaphoreType.DMA
    out = pl.pallas_call(
        kernel,
        out_shape=pltpu.VMEM((CH, NZ, NY, NX), F32),
        in_specs=[pl.BlockSpec(memory_space=pl.ANY)] * 15,
        out_specs=vmem,
        scratch_shapes=[
            pltpu.VMEM((CH, NZ, NY, NX), F32), pltpu.VMEM((CH, NZ, NY, NX), BF16),
            pltpu.VMEM((27 * CH, FT), BF16), pltpu.VMEM((27 * FT, FT), BF16), pltpu.VMEM((27 * CH, FT), BF16),
            pltpu.SMEM((1, FT), F32), pltpu.SMEM((1,), F32), pltpu.SMEM((1,), F32), *params, pltpu.SMEM((CH,), F32),
            pltpu.VMEM((2, NZ + 2 * HALO, 4, 16, NX), BF16),
            pltpu.VMEM((192, (NZ + 2 * HALO) * NX), BF16),
            pltpu.VMEM((256, 8 * NX), F32),
            pltpu.VMEM((256, 8 * NX), BF16),
            pltpu.VMEM((256, 6 * NX), F32),
            pltpu.VMEM((256, 6 * NX), BF16),
            pltpu.VMEM((256, 576), BF16),
            pltpu.VMEM((768, 768), BF16),
            pltpu.VMEM((192, 768), BF16),
            pltpu.VMEM((864, 256), F32),
            pltpu.VMEM((6, 256, NX), F32),
            pltpu.VMEM((64, NX), F32),
            pltpu.VMEM((NZ, 64, NX), F32),
            pltpu.VMEM((4, 1, NX), F32),
            pltpu.VMEM((4, SIDE, 1, NX), F32),
            pltpu.VMEM((3, HALF, 4, NY, NX), F32),
            pltpu.VMEM((HALF, 4, NY, NX), F32),
            pltpu.VMEM((2, HALF, 4, NY, NX), F32),
            pltpu.VMEM((HALF, 2, 16, NX), BF16),
            pltpu.VMEM((2, 4, NY, NX), F32),
            pltpu.VMEM((2, 4, NY, NX), F32),
            pltpu.SemaphoreType.REGULAR((4,)), dma((15,)), dma((2, 2)), dma((2, 2)), dma((HALF,)), dma((4,)), dma((4, SIDE)), dma((4, SIDE)),
            dma((2, HALF)), dma((2, HALF)), dma((2, HALF)), dma((2, HALF)), dma((2,)), dma((2,)),
        ],
        compiler_params=pltpu.CompilerParams(
            collective_id=0, has_side_effects=True, vmem_limit_bytes=60 * 2**20
        ),
    )(
        latent_start, noise_draws[0], time_embed, step_scale, noise_scale,
        w_in.transpose(2, 3, 4, 1, 0).reshape(27 * CH, FT), b_in, gain_in, shift_in,
        w_mid.transpose(2, 3, 4, 0, 1).reshape(27 * FT, FT), b_mid, gain_mid, shift_mid,
        w_out.transpose(2, 3, 4, 0, 1).reshape(27 * CH, FT), b_out,
    )
    return out[None]


def solution(mesh):
    in_specs = (
        P(None, "gz", None, None), P("tm", None, "gz", None, None), P("tm", None), P("tm"), P("tm"),
        P(), P(), P(), P(), P(), P(), P(), P(), P(), P(),
    )
    out_specs = P("tm", None, "gz", None, None)
    return jax.shard_map(shards, mesh=mesh, in_specs=in_specs, out_specs=out_specs, check_vma=False)
```

```python
import functools

import jax
import jax.numpy as jnp
from jax import lax
from jax.experimental import pallas as pl
from jax.experimental.pallas import tpu as pltpu
from jax.sharding import PartitionSpec as P

MESH = pl.DeviceIdType.MESH
F32, BF16 = jnp.float32, jnp.bfloat16
CH, FT, GR = 8, 32, 8
NY, NX, NZ = 8, 128, 4
SIDE = 16
HALO = 3
CELLS = (FT // GR) * NZ * NY * NX

GZ_ORDER = (12, 13, 4, 5, 8, 9, 14, 15, 10, 11, 2, 3, 6, 7, 1)
HALF = 8
HALF_ORDER = (7, 5, 6, 3, 4, 1, 2)


def flip(place, bits):
    for bit in (1, 2, 4, 8):
        if bits & bit:
            place = place + bit - 2 * bit * lax.rem(lax.div(place, bit), 2)
    return place


def unfold(count):
    row = lax.broadcasted_iota(jnp.int32, (count, 8 * count), 0)
    lane = lax.broadcasted_iota(jnp.int32, (count, 8 * count), 1)
    return (lax.div(lane, 8) == row).astype(F32).astype(BF16)


def tap_masks(lanes):
    y = lax.broadcasted_iota(jnp.int32, (8, lanes), 0)
    yin = lax.rem(lax.broadcasted_iota(jnp.int32, (8, lanes), 1), 8)
    return [yin == lax.rem(y + b + 7, 8) for b in range(3)]


def circulant(rows, masks):
    n, lanes = rows[0].shape
    out = jnp.zeros((n, 8, lanes), F32)
    for row, mask in zip(rows, masks):
        full = jnp.broadcast_to(row[:, None, :], (n, 8, lanes))
        out = jnp.where(jnp.broadcast_to(mask[None], (n, 8, lanes)), full, out)
    return out.reshape(8 * n, lanes)


def kernel(
    lat_hbm, noise_hbm, emb_hbm, step_hbm, nsc_hbm, win_hbm, bin_hbm, gin_hbm, sin_hbm,
    wmid_hbm, bmid_hbm, gmid_hbm, smid_hbm, wout_hbm, bout_hbm,
    out_ref,
    lat_ref, noise_ref, win_ref, wmid_ref, wout_ref, emb_ref, step_ref, nsc_ref,
    bin_ref, gin_ref, sin_ref, bmid_ref, gmid_ref, smid_ref, bout_ref,
    vext, shift_in, lifted, act, summed, actb, a_in, a_mid, a_out, x_mid, splat, splat_out, drift,
    stat, recv, send1, lat_chunk, chunk_a, chunk_b, half_sum, earlier_sum,
    relay_sem, load_sem, halo_ss, halo_rs, edge_ss, edge_rs, stat_ss, stat_rs, p1_ss, p1_rs, p2_ss, p2_rs, sum_ss, sum_rs,
):
    k = lax.axis_index("tm")
    g = lax.axis_index("gz")
    up, down = lax.rem(g + 1, SIDE), lax.rem(g + SIDE - 1, SIDE)
    gz_peers = [flip(g, bits) for bits in GZ_ORDER]
    tm_peers = [flip(k, bits) for bits in HALF_ORDER]
    late, place = lax.div(k, HALF), lax.rem(k, HALF)
    twin = flip(k, HALF + 4)

    def owned(device):
        at = lax.rem(device, HALF)
        return at + late * (4 - 8 * lax.div(at, 4))

    mine = owned(k)
    my_z, my_p = lax.div(mine, 2), lax.rem(mine, 2)
    pending = []

    barrier = pltpu.get_barrier_semaphore()
    beside, across = [flip(k, 2), flip(k, 4)], [flip(k, 1)]
    for peer in beside + across:
        pl.semaphore_signal(barrier, inc=1, device_id={"tm": peer}, device_id_type=MESH)
    for peer in gz_peers[2:]:
        pl.semaphore_signal(barrier, inc=1, device_id={"gz": peer}, device_id_type=MESH)

    @pl.when(late == 0)
    def _():
        pl.semaphore_signal(barrier, inc=1, device_id={"tm": twin}, device_id_type=MESH)

    loads = []
    for src, dst in (
        (lat_hbm, lat_ref), (wmid_hbm, wmid_ref), (wout_hbm, wout_ref), (win_hbm, win_ref), (emb_hbm, emb_ref),
        (bin_hbm, bin_ref), (gin_hbm, gin_ref), (sin_hbm, sin_ref), (bmid_hbm, bmid_ref), (gmid_hbm, gmid_ref),
        (smid_hbm, smid_ref), (bout_hbm, bout_ref), (step_hbm, step_ref), (nsc_hbm, nsc_ref), (noise_hbm, noise_ref),
    ):
        copy = pltpu.make_async_copy(src, dst, load_sem.at[len(loads)])
        copy.start()
        loads.append(copy)

    loads[0].wait()
    for z in range(NZ):
        plane = lat_ref[:, z].reshape(CH * NY, NX)
        vext[0, HALO + z] = plane.reshape(4, 16, NX).astype(BF16)
        lat_chunk[2 * z : 2 * z + 2] = plane.reshape(2, 4, NY, NX)

    pl.semaphore_wait(barrier, len(GZ_ORDER) - 2 + len(beside + across) + late)

    def relay(turn, peers):
        for peer in peers:
            pl.semaphore_signal(relay_sem.at[turn], inc=1, device_id={"tm": peer}, device_id_type=MESH)

    relay(0, beside)
    pl.semaphore_signal(relay_sem.at[3], inc=1, device_id={"gz": flip(g, 4)}, device_id_type=MESH)

    @pl.when(late == 1)
    def _():
        relay(2, [twin])

    @pl.when(late == 0)
    def _():
        earlier_sum[...] = jnp.zeros_like(earlier_sum)

    def send(src, dst, ss, rs, device):
        copy = pltpu.make_async_remote_copy(
            src_ref=src, dst_ref=dst, send_sem=ss, recv_sem=rs, device_id=device, device_id_type=MESH
        )
        copy.start()
        pending.append(copy)
        return copy

    def settle(copies):
        fresh = {id(copy) for copy in copies}
        for copy in pending:
            if id(copy) not in fresh:
                copy.wait_send()
        pending[:] = copies
        for copy in copies:
            copy.wait_recv()

    halo = [
        send(vext.at[0, pl.ds(NZ, HALO)], vext.at[0, pl.ds(0, HALO)],
             halo_ss.at[0, 0], halo_rs.at[0, 0], {"gz": up}),
        send(vext.at[0, pl.ds(HALO, HALO)], vext.at[0, pl.ds(HALO + NZ, HALO)],
             halo_ss.at[0, 1], halo_rs.at[0, 1], {"gz": down}),
    ]

    def load_mid():
        loads[1].wait()
        x_mid[...] = jnp.dot(wmid_ref[...], unfold(FT), preferred_element_type=F32)
        masks = tap_masks(256)
        for a in range(3):
            for block in range(12):
                first = a * 288 + 8 * block
                rows = [x_mid[first + 96 * b : first + 96 * b + 8, :] for b in range(3)]
                a_mid[64 * block : 64 * block + 64, 256 * a : 256 * a + 256] = circulant(rows, masks).astype(BF16)

    def load_out():
        loads[2].wait()
        masks = tap_masks(256)
        x_out = jnp.dot(wout_ref[...], unfold(FT), preferred_element_type=F32)
        for a in range(3):
            rows = [x_out[(a * 3 + b) * 24 : (a * 3 + b) * 24 + 24] for b in range(3)]
            a_out[:, 256 * a : 256 * a + 256] = circulant(rows, masks).astype(BF16)

    loads[3].wait()
    masks = tap_masks(576)
    rows = []
    for b in range(3):
        w_b = jnp.concatenate([win_ref[(a * 3 + b) * 24 : (a * 3 + b) * 24 + 24, :].astype(F32) for a in range(3)], axis=0)
        rows.append(jnp.dot(w_b.T.astype(BF16), unfold(72), preferred_element_type=F32))
    for block in range(4):
        part = [row[8 * block : 8 * block + 8] for row in rows]
        a_in[64 * block : 64 * block + 64, :] = circulant(part, masks).astype(BF16)

    for copy in loads[4:]:
        copy.wait()

    def spread(o, carry):
        at = pl.ds(pl.multiple_of(o * 8, 8), 8)
        for i, value in enumerate((
            bin_ref[o] + emb_ref[0, o], 0.5 * gin_ref[o], 0.5 * sin_ref[o],
            bmid_ref[o], 0.5 * gmid_ref[o], 0.5 * smid_ref[o],
        )):
            splat[i, at, :] = jnp.full((8, NX), value, F32)
        return carry

    lax.fori_loop(0, FT, spread, 0)
    for o in range(CH):
        splat_out[8 * o : 8 * o + 8, :] = jnp.full((8, NX), bout_ref[o], F32)
    step, noise_scale = step_ref[0], nsc_ref[0]

    def lanes(first, count=1):
        return slice(NX * first, NX * (first + count))

    sub = lax.broadcasted_iota(jnp.int32, (8, NX), 0)
    lane = lax.broadcasted_iota(jnp.int32, (8, NX), 1)
    own_lane, first_lane = lax.rem(lane, GR) == sub, lane == sub

    def lane_sums(groups):
        rows = jnp.concatenate([jnp.sum(t, axis=0, keepdims=True) for t in groups], axis=0)
        return jnp.broadcast_to(jnp.sum(rows, axis=1, keepdims=True), (8, NX))

    def fold(ref, planes, centre=None):
        plain, squares = [], []
        for gr in range(GR):
            tiles = []
            for q in planes:
                for c in range(4):
                    tile = ref[32 * gr + 8 * c : 32 * gr + 8 * c + 8, lanes(q)]
                    tiles.append(tile if centre is None else tile - jnp.broadcast_to(centre[gr : gr + 1], (8, NX)))
            plain.append(functools.reduce(lambda x, y: x + y, tiles))
            if centre is not None:
                squares.append(functools.reduce(lambda x, y: x + y, [t * t for t in tiles]))
        return plain, squares

    def centre_of(ref, planes):
        return lane_sums(fold(ref, planes)[0]) * (1.0 / (len(planes) * 4 * NY * NX))

    def announce(ref, inner, outer, centre, turn):
        plain, squares = fold(ref, inner, centre)
        plain2, squares2 = fold(ref, outer, centre)
        first = lane_sums([x + y for x, y in zip(plain, plain2)])
        second = lane_sums([x + y for x, y in zip(squares, squares2)])
        off = first * (1.0 / CELLS)
        both = jnp.where(lax.rem(lane, 2 * GR) < GR, centre + off, second - first * off)
        row = jnp.sum(jnp.where(own_lane, both, 0.0), axis=0, keepdims=True)
        stat[turn] = row
        recv[turn, g] = row
        return [
            send(stat.at[turn], recv.at[turn, g], stat_ss.at[turn, i], stat_rs.at[turn, i], {"gz": peer})
            for i, peer in enumerate(gz_peers)
        ]

    def gathered(copies, turn):
        settle(copies)
        every = recv[turn]
        total = jnp.sum(every, axis=0)
        mean = total * (1.0 / SIDE)
        off = every - mean[None]
        spread_of = jnp.sum(off * off, axis=0)
        var = (pltpu.roll(total, NX - GR, 1) + spread_of * CELLS) * (1.0 / (CELLS * SIDE))

        def by_row(row):
            picked = jnp.where(first_lane, jnp.broadcast_to(row, (8, NX)), 0.0)
            return jnp.broadcast_to(jnp.sum(picked, axis=1, keepdims=True), (8, NX))

        return by_row(mean), by_row(lax.rsqrt(var + 1e-05))

    def activate(src, dst, planes, mean, inv, gain, shift):
        for gr in range(GR):
            at = slice(32 * gr, 32 * gr + 32)
            m = jnp.broadcast_to(mean[gr : gr + 1], (32, NX))
            f = jnp.broadcast_to(inv[gr : gr + 1], (32, NX)) * splat[gain, at, :]
            s = splat[shift, at, :]
            for q in planes:
                half = (src[at, lanes(q)] - m) * f + s
                dst[at, lanes(q)] = (half + half * jnp.tanh(half)).astype(BF16)

    def stack(src, planes):
        return jnp.concatenate([jnp.concatenate([src[:, lanes(q + a)] for q in planes], axis=1) for a in range(3)], axis=0)

    def turned(sweep, planes):
        for e in planes:
            plane = vext[sweep, e].reshape(CH * NY, NX)
            wide = plane.astype(F32)
            shift_in[0:64, lanes(e)] = pltpu.roll(wide, 1, 1).astype(BF16)
            shift_in[64:128, lanes(e)] = plane
            shift_in[128:192, lanes(e)] = pltpu.roll(wide, NX - 1, 1).astype(BF16)

    def lift(planes):
        out = jnp.dot(a_in[...], stack(shift_in, planes), preferred_element_type=F32)
        for i, q in enumerate(planes):
            lifted[:, lanes(q)] = out[:, lanes(i)] + splat[0]

    def middle(planes):
        rhs = stack(act, planes)
        taps = [jnp.dot(a_mid[256 * c : 256 * c + 256, :], rhs, preferred_element_type=F32) for c in range(3)]
        for i, r in enumerate(planes):
            summed[:, lanes(r)] = (
                pltpu.roll(taps[0][:, lanes(i)], 1, 1) + taps[1][:, lanes(i)]
                + pltpu.roll(taps[2][:, lanes(i)], NX - 1, 1) + splat[3] + lifted[:, lanes(r + 1)]
            )

    for sweep in range(2):
        if sweep == 0:
            for z in range(NZ):
                draws = noise_ref[:, z].astype(F32).reshape(CH * NY, NX)
                drift[z] = step * splat_out[...] + noise_scale * draws
            turned(sweep, (3, 4, 5, 6))
            lift((3, 4))
            centre = centre_of(lifted, (3, 4))
            settle(halo)
            turned(sweep, (2, 7))
            lift((2, 5))
            pl.semaphore_wait(relay_sem.at[3], 1)
            copies = announce(lifted, (3, 4), (2, 5), centre, 0)
            pl.semaphore_wait(relay_sem.at[0], 2)
            relay(1, across)
            turned(sweep, (0, 1, 8, 9))
            lift((0, 1, 6, 7))
            load_mid()
        else:
            halo = [
                send(vext.at[1, pl.ds(NZ, 2)], vext.at[1, pl.ds(0, 2)],
                     halo_ss.at[1, 0], halo_rs.at[1, 0], {"gz": up}),
                send(vext.at[1, pl.ds(NZ, 2)], vext.at[1, pl.ds(HALO + NZ + 1, 2)],
                     halo_ss.at[1, 1], halo_rs.at[1, 1], {"gz": down}),
            ]
            turned(sweep, (2, 3, 4, 5, 6, 7))
            lift((3, 4))
            centre = centre_of(lifted, (3, 4))
            lift((2, 5))
            copies = announce(lifted, (3, 4), (2, 5), centre, 2)
            for copy in halo:
                copy.wait_recv()
            turned(sweep, (0, 1, 8, 9))
            lift((0, 1, 6, 7))
        mean, inv = gathered(copies, 2 * sweep)
        if sweep == 0:
            pl.semaphore_wait(relay_sem.at[1], 1)

        activate(lifted, act, (1, 2, 3, 4, 5, 6), mean, inv, 1, 2)
        middle((2, 3))
        centre = centre_of(summed, (2, 3))
        middle((1, 4))
        copies = announce(summed, (2, 3), (1, 4), centre, 2 * sweep + 1)
        activate(lifted, act, (0, 7), mean, inv, 1, 2)
        middle((0, 5))
        if sweep == 0:
            load_out()
        mean, inv = gathered(copies, 2 * sweep + 1)

        activate(summed, actb, range(6), mean, inv, 4, 5)
        taps = jnp.dot(a_out[...], stack(actb, range(NZ)), preferred_element_type=F32)
        for z in range(NZ):
            predicted = (
                pltpu.roll(taps[0:64, lanes(z)], 1, 1) + taps[64:128, lanes(z)]
                + pltpu.roll(taps[128:192, lanes(z)], NX - 1, 1)
            )
            send1[sweep, 2 * z : 2 * z + 2] = (step * predicted + drift[z]).reshape(2, 4, NY, NX)

        chunk_a[sweep, place] = send1[sweep, mine]
        copies = [
            send(send1.at[sweep, owned(peer)], chunk_a.at[sweep, place],
                 p1_ss.at[sweep, i], p1_rs.at[sweep, i], {"tm": peer})
            for i, peer in enumerate(tm_peers)
        ]
        settle(copies)

        def onward():
            return pltpu.make_async_remote_copy(
                src_ref=half_sum.at[sweep], dst_ref=earlier_sum.at[sweep], send_sem=sum_ss.at[sweep],
                recv_sem=sum_rs.at[sweep], device_id={"tm": twin}, device_id_type=MESH,
            )

        @pl.when(late == 0)
        def _():
            half_sum[sweep] = jnp.sum(chunk_a[sweep], axis=0)
            if sweep == 0:
                pl.semaphore_wait(relay_sem.at[2], 1)
            onward().start()

        @pl.when(late == 1)
        def _():
            onward().wait_recv()

        state = lat_chunk[mine] + earlier_sum[sweep]
        for s in range(HALF):
            if sweep == 0:
                chunk_b[s] = state.reshape(2, 16, NX).astype(BF16)
            state = state + chunk_a[sweep, s]
            if sweep == 1:
                send1[2, s] = state
        copies = []
        if sweep == 0:
            face = (my_z == 0) | (my_z == NZ - 1)
            first = my_z == 0
            other, plane = jnp.where(first, down, up), jnp.where(first, HALO + NZ, HALO - 1)
            edge = jnp.where(first, 2, 0) + my_p

            def edge_copy(i, peer):
                return pltpu.make_async_remote_copy(
                    src_ref=chunk_b.at[lax.rem(peer, HALF)], dst_ref=vext.at[1, plane, pl.ds(2 * my_p, 2)],
                    send_sem=edge_ss.at[i], recv_sem=edge_rs.at[edge],
                    device_id={"tm": peer, "gz": other}, device_id_type=MESH,
                )

        for i, peer in enumerate(tm_peers):
            if sweep == 0:
                src, dst = chunk_b.at[lax.rem(peer, HALF)], vext.at[1, HALO + my_z, pl.ds(2 * my_p, 2)]
            else:
                src, dst = send1.at[2, lax.rem(peer, HALF)], out_ref.at[pl.ds(4 * my_p, 4), my_z]
            copies.append(send(src, dst, p2_ss.at[sweep, i], p2_rs.at[sweep, i], {"tm": peer}))
        if sweep == 0:

            @pl.when(face)
            def _():
                for i, peer in enumerate(tm_peers + [k]):
                    edge_copy(i, peer).start()

            vext[1, HALO + my_z, pl.ds(2 * my_p, 2)] = chunk_b[place]
        else:
            out_ref[pl.ds(4 * my_p, 4), my_z] = send1[2, place]
        settle(copies)
        if sweep == 0:
            for i in range(4):
                pltpu.make_async_remote_copy(
                    src_ref=chunk_b.at[0],
                    dst_ref=vext.at[1, HALO + NZ if i >= 2 else HALO - 1, pl.ds(2 * (i % 2), 2)],
                    send_sem=edge_ss.at[0], recv_sem=edge_rs.at[i], device_id={"gz": up}, device_id_type=MESH,
                ).wait_recv()

            @pl.when(face)
            def _():
                for i, peer in enumerate(tm_peers + [k]):
                    edge_copy(i, peer).wait_send()

        @pl.when(late == 0)
        def _():
            onward().wait_send()

    for copy in pending:
        copy.wait_send()


def shards(
    latent_start, noise_draws, time_embed, step_scale, noise_scale, w_in, b_in, gain_in, shift_in,
    w_mid, b_mid, gain_mid, shift_mid, w_out, b_out,
):
    vmem = pl.BlockSpec(memory_space=pltpu.VMEM)
    params = [pltpu.SMEM((FT,), F32)] * 6
    dma = pltpu.SemaphoreType.DMA
    out = pl.pallas_call(
        kernel,
        out_shape=pltpu.VMEM((CH, NZ, NY, NX), F32),
        in_specs=[pl.BlockSpec(memory_space=pl.ANY)] * 15,
        out_specs=vmem,
        scratch_shapes=[
            pltpu.VMEM((CH, NZ, NY, NX), F32), pltpu.VMEM((CH, NZ, NY, NX), BF16),
            pltpu.VMEM((27 * CH, FT), BF16), pltpu.VMEM((27 * FT, FT), BF16), pltpu.VMEM((27 * CH, FT), BF16),
            pltpu.SMEM((1, FT), F32), pltpu.SMEM((1,), F32), pltpu.SMEM((1,), F32), *params, pltpu.SMEM((CH,), F32),
            pltpu.VMEM((2, NZ + 2 * HALO, 4, 16, NX), BF16),
            pltpu.VMEM((192, (NZ + 2 * HALO) * NX), BF16),
            pltpu.VMEM((256, 8 * NX), F32),
            pltpu.VMEM((256, 8 * NX), BF16),
            pltpu.VMEM((256, 6 * NX), F32),
            pltpu.VMEM((256, 6 * NX), BF16),
            pltpu.VMEM((256, 576), BF16),
            pltpu.VMEM((768, 768), BF16),
            pltpu.VMEM((192, 768), BF16),
            pltpu.VMEM((864, 256), F32),
            pltpu.VMEM((6, 256, NX), F32),
            pltpu.VMEM((64, NX), F32),
            pltpu.VMEM((NZ, 64, NX), F32),
            pltpu.VMEM((4, 1, NX), F32),
            pltpu.VMEM((4, SIDE, 1, NX), F32),
            pltpu.VMEM((3, HALF, 4, NY, NX), F32),
            pltpu.VMEM((HALF, 4, NY, NX), F32),
            pltpu.VMEM((2, HALF, 4, NY, NX), F32),
            pltpu.VMEM((HALF, 2, 16, NX), BF16),
            pltpu.VMEM((2, 4, NY, NX), F32),
            pltpu.VMEM((2, 4, NY, NX), F32),
            pltpu.SemaphoreType.REGULAR((4,)), dma((15,)), dma((2, 2)), dma((2, 2)), dma((HALF,)), dma((4,)), dma((4, SIDE)), dma((4, SIDE)),
            dma((2, HALF)), dma((2, HALF)), dma((2, HALF)), dma((2, HALF)), dma((2,)), dma((2,)),
        ],
        compiler_params=pltpu.CompilerParams(
            collective_id=0, has_side_effects=True, vmem_limit_bytes=60 * 2**20
        ),
    )(
        latent_start, noise_draws[0], time_embed, step_scale, noise_scale,
        w_in.transpose(2, 3, 4, 1, 0).reshape(27 * CH, FT), b_in, gain_in, shift_in,
        w_mid.transpose(2, 3, 4, 0, 1).reshape(27 * FT, FT), b_mid, gain_mid, shift_mid,
        w_out.transpose(2, 3, 4, 0, 1).reshape(27 * CH, FT), b_out,
    )
    return out[None]


def solution(mesh):
    in_specs = (
        P(None, "gz", None, None), P("tm", None, "gz", None, None), P("tm", None), P("tm"), P("tm"),
        P(), P(), P(), P(), P(), P(), P(), P(), P(), P(),
    )
    out_specs = P("tm", None, "gz", None, None)
    return jax.shard_map(shards, mesh=mesh, in_specs=in_specs, out_specs=out_specs, check_vma=False)
```
